256 devices in a mesh: engine: 32 (over x, z_hi, y), tensor: 8 (over z_lo, core).
Axes of the slice: x: 4, y: 4, z: 8 (z_hi: 2, z_lo: 4; z = z_hi * 4 + z_lo), core: 2. Of those that a mesh axis runs over, the one named last changes fastest.
Arguments:
- token_states: bfloat16 [512, 20, 5120], P('engine', None, 'tensor'), may hold values from -6 to 6
- row_len: int32 [512], P('engine'), may hold values from 1 to 20
- row_dest: int32 [512], P('engine'), may hold values from 0 to 31, as said below
- norm_gain: float32 [2, 5120], replicated, may hold values from 0.1 to 1.9
- q_gain: float32 [128], replicated, may hold values from 0.1 to 1.9
- k_gain: float32 [2, 128], replicated, may hold values from 0.1 to 1.9
- q_weight: bfloat16 [5120, 4096], P('engine', 'tensor'), may hold values from -0.078125 to 0.078125
- kv_weight0: bfloat16 [5120, 2, 1024], P('engine', None, 'tensor'), may hold values from -0.078125 to 0.078125
- out_weight: bfloat16 [5120, 4096], P('engine', 'tensor'), may hold values from -0.09375 to 0.09375
- kv_weight1: bfloat16 [5120, 2, 1024], P('engine', None, 'tensor'), may hold values from -0.078125 to 0.078125
Outputs:
- caches: bfloat16 [2, 2, 1024, 20, 1024], P(None, None, 'engine', None, 'tensor')
The draws below stay inside these ranges and needn't reach their ends.
Inputs may be any that keep to these rules, and one draw needn't show every extreme that they name: `row_dest`: every engine receives 0, 16 or 32 rows: a quarter of the engines 2 * 16, a half 16. No engine sends more than 1 row to one engine.
All inputs are finite; a program needn't handle non-finite values.
Results may differ from the reference program's by a relative error of at most 0.012.
Values may be sent and summed in bfloat16 or wider, within the bound.
A program may use at most 128 MiB of HBM per device.

```python
import jax
import jax.numpy as jnp
from jax import lax

D = 5120
HQ = 32
KVH = 8
HD = 128
LMAX = 20
ROWS_DEV = 16
ROWS = 512
N_ENGINE = 32
N_TENSOR = 8


def draw_row_dest(key, part):
    key = jax.random.fold_in(key, 7)
    label_key, order_key = jax.random.split(key)
    engines = N_ENGINE
    quarter = engines // 4
    labels = jax.random.permutation(label_key, engines).astype(jnp.int32)
    sources = jnp.arange(engines, dtype=jnp.int32)[:, None]
    steps_in = jnp.arange(quarter, dtype=jnp.int32)[None, :]
    heavy = jnp.broadcast_to(jnp.arange(quarter, dtype=jnp.int32)[None, :], (engines, quarter))
    middle = quarter + (sources + steps_in) % (2 * quarter)
    classes = jnp.concatenate([heavy, middle], axis=1)
    targets = labels[classes]
    row_keys = jax.random.split(order_key, engines)
    shuffled = jax.vmap(lambda one_key, one_row: jax.random.permutation(one_key, one_row))(row_keys, targets)
    return shuffled.reshape(-1).astype(jnp.int32)


def set_ends(values, stream_key, smallest, high):
    index_at = [jax.random.randint(jax.random.fold_in(stream_key, axis), (), 0, length) for axis, length in enumerate(values.shape)]
    main_axis = values.shape.index(max(values.shape))
    beside = index_at[:main_axis] + [(index_at[main_axis] + 1) % values.shape[main_axis]] + index_at[main_axis + 1:]
    return values.at[tuple(index_at)].set(smallest).at[tuple(beside)].set(high)


def block_scale(rng, dims, cuts, low, top_value):
    factor_of, own = 1.0, jax.random.fold_in(rng, 6)
    for dim, blocks in cuts:
        steps = jnp.exp(jax.random.uniform(jax.random.fold_in(own, dim), (blocks,), jnp.float32, low / len(cuts), top_value / len(cuts)))
        factor_of = factor_of * jnp.repeat(steps, dims[dim] // blocks).reshape([-1 if axis == dim else 1 for axis in range(len(dims))])
    return factor_of


def normal_values(key, extent, width, most, cuts=(), kind=jnp.bfloat16):
    factor_of = block_scale(key, extent, cuts, -0.22, 0.18) if cuts else 1.0
    entries = jax.random.normal(key, extent, jnp.float32) * width * factor_of
    return jnp.minimum(jnp.maximum(entries, -most), most).astype(kind)


def setup_inputs(seed: int = 0) -> dict:
    arg_keys = jax.random.split(jax.random.key(seed), 11)
    token_states = normal_values(arg_keys[0], (ROWS, LMAX, D), 1.0, 6.0, ((0, 32), (2, 8)))
    row_len = set_ends(jax.random.randint(arg_keys[1], (ROWS,), 1, LMAX + 1), jax.random.fold_in(arg_keys[1], 1), 1, LMAX).astype(jnp.int32)
    row_dest = draw_row_dest(jax.random.fold_in(arg_keys[10], 71), 0)
    norm_gain = jnp.clip(1.0 + 0.18 * jax.random.normal(arg_keys[3], (2, D), jnp.float32), 0.1, 1.9)
    q_gain = jnp.clip(1.0 + 0.18 * jax.random.normal(arg_keys[4], (HD,), jnp.float32), 0.1, 1.9)
    k_gain = jnp.clip(1.0 + 0.18 * jax.random.normal(arg_keys[5], (2, HD), jnp.float32), 0.1, 1.9)
    q_weight = normal_values(arg_keys[6], (D, HQ * HD), D ** -0.5, 0.078125, ((0, 32), (1, 8)))
    kv_weight0 = normal_values(arg_keys[7], (D, 2, KVH * HD), D ** -0.5, 0.078125, ((0, 32), (2, 8)))
    out_weight = normal_values(arg_keys[8], (D, HQ * HD), (HQ * HD) ** -0.5, 0.09375, ((0, 32), (1, 8)))
    kv_weight1 = normal_values(arg_keys[9], (D, 2, KVH * HD), D ** -0.5, 0.078125, ((0, 32), (2, 8)))
    return {"token_states": token_states, "row_len": row_len, "row_dest": row_dest, "norm_gain": norm_gain, "q_gain": q_gain, "k_gain": k_gain, "q_weight": q_weight, "kv_weight0": kv_weight0, "out_weight": out_weight, "kv_weight1": kv_weight1}


NORM_EPSILON = 1e-06
ROTARY_BASE = 1000000.0

def root_norm(values, gain_row):
    return values * lax.rsqrt(lax.optimization_barrier(jnp.mean(values * values, axis=-1, keepdims=True)) + NORM_EPSILON) * gain_row

def rotary(values, positions):
    half_dim = values.shape[-1] // 2
    frequency = jnp.power(ROTARY_BASE, -jnp.arange(half_dim, dtype=jnp.float32) * 2.0 / (2 * half_dim))
    angles = positions.astype(jnp.float32)[:, None] * frequency[None, :]
    cosine = jnp.cos(angles)[:, None, :]
    sine_part = jnp.sin(angles)[:, None, :]
    lower_half = values[..., :half_dim]
    upper_half = values[..., half_dim:]
    return jnp.concatenate([lower_half * cosine - upper_half * sine_part, upper_half * cosine + lower_half * sine_part], axis=-1)

def attend(queries, keys_in, values_in):
    span = queries.shape[1]
    head_dim = queries.shape[-1]
    scores = jnp.einsum('nikgd,njkd->nkgij', queries.astype(jnp.float32), keys_in.astype(jnp.float32)) / jnp.sqrt(jnp.float32(head_dim))
    causal = jnp.arange(span)[:, None] >= jnp.arange(span)[None, :]
    weights = jnp.where(causal, jnp.exp(scores), jnp.float32(0.0))
    probabilities = (weights / lax.optimization_barrier(jnp.sum(weights, axis=-1, keepdims=True))).astype(jnp.bfloat16)
    result = jnp.einsum('nkgij,njkd->nikgd', probabilities.astype(jnp.float32), values_in.astype(jnp.float32))
    return result.astype(jnp.bfloat16)

def reference(token_states, row_len, row_dest, norm_gain, q_gain, k_gain, q_weight, kv_weight0, out_weight, kv_weight1):
    row_total, row_span, model_width = token_states.shape
    head_dim = q_gain.shape[0]
    cache_width = kv_weight0.shape[2]
    cache_heads = cache_width // head_dim
    query_heads = q_weight.shape[1] // head_dim
    group_size = query_heads // cache_heads
    positions = jnp.arange(row_span, dtype=jnp.int32)
    flat_rows = token_states.reshape(row_total * row_span, model_width).astype(jnp.float32)
    normed0 = root_norm(flat_rows, norm_gain[0]).astype(jnp.bfloat16)
    queries = jnp.dot(normed0, q_weight, preferred_element_type=jnp.float32)
    key_value = jnp.dot(normed0, kv_weight0.reshape(model_width, 2 * cache_width), preferred_element_type=jnp.float32)
    key_value = key_value.reshape(row_total, row_span, 2, cache_heads, head_dim)
    queries = rotary(root_norm(queries.reshape(row_total, row_span, query_heads, head_dim), q_gain), positions).astype(jnp.bfloat16)
    first_keys = rotary(root_norm(key_value[:, :, 0], k_gain[0]), positions).astype(jnp.bfloat16)
    first_values = key_value[:, :, 1].astype(jnp.bfloat16)
    attended = attend(queries.reshape(row_total, row_span, cache_heads, group_size, head_dim), first_keys, first_values)
    attended = attended.reshape(row_total * row_span, query_heads * head_dim)
    group_cols = query_heads * head_dim // N_TENSOR
    summed = jnp.zeros((row_total * row_span, model_width), jnp.float32)
    for member in range(N_TENSOR):
        lower = member * group_cols
        partial_value = jnp.dot(attended[:, lower:lower + group_cols], out_weight[:, lower:lower + group_cols].T, preferred_element_type=jnp.float32).astype(jnp.bfloat16)
        summed = summed + lax.optimization_barrier(partial_value).astype(jnp.float32)
    hidden = flat_rows + summed
    normed1 = root_norm(hidden, norm_gain[1]).astype(jnp.bfloat16)
    second_pair = jnp.dot(normed1, kv_weight1.reshape(model_width, 2 * cache_width), preferred_element_type=jnp.float32)
    second_pair = second_pair.reshape(row_total, row_span, 2, cache_heads, head_dim)
    second_keys = rotary(root_norm(second_pair[:, :, 0], k_gain[1]), positions).astype(jnp.bfloat16)
    second_values = second_pair[:, :, 1].astype(jnp.bfloat16)
    stacked = jnp.stack([first_keys, first_values, second_keys, second_values], axis=2).reshape(row_total, row_span, 4, cache_width)
    live_mask = positions[None, :] < row_len[:, None]
    stacked = jnp.where(live_mask[:, :, None, None], stacked, jnp.zeros((), jnp.bfloat16))
    slot_count = 2 * ROWS_DEV
    onehot = (row_dest[:, None] == jnp.arange(N_ENGINE, dtype=jnp.int32)[None, :]).astype(jnp.int32)
    before = jnp.cumsum(onehot, axis=0) - onehot
    slot_index = lax.optimization_barrier(jnp.sum(before * onehot, axis=1)).astype(jnp.int32)
    target = (row_dest * slot_count + slot_index).astype(jnp.int32)
    placed = jnp.zeros((N_ENGINE * slot_count, row_span, 4, cache_width), jnp.bfloat16).at[target].set(stacked)
    return placed.reshape(N_ENGINE * slot_count, row_span, 2, 2, cache_width).transpose(2, 3, 0, 1, 4)
```

```python
import functools

import jax
import jax.numpy as jnp
import numpy as np
from jax import lax
from jax.experimental import pallas as pl
from jax.experimental.pallas import tpu as pltpu
from jax.sharding import PartitionSpec as P

EPS = 1e-06
ROTARY_BASE = 1000000.0
MESH = pl.DeviceIdType.MESH
TOK = 320
SPAN = 20
WC = 768
CB = 80
F32 = jnp.float32
BF = jnp.bfloat16
NT = (((1,), (1,)), ((), ()))


def mod4(v):
    return lax.rem(v + 8, 4)


def device(x, y, z, c):
    z = lax.rem(z + 16, 8)
    return (mod4(x) * 8 + (z // 4) * 4 + mod4(y), lax.rem(z, 4) * 2 + c)


def rcopy(src, dst, send_sem, recv_sem, target):
    return pltpu.make_async_remote_copy(
        src_ref=src, dst_ref=dst, send_sem=send_sem, recv_sem=recv_sem,
        device_id=target, device_id_type=MESH,
    )


def rope(v, cos, sin):
    return v * cos + pltpu.roll(v, 64, 1) * sin


def head_norm(v, gain):
    return v * lax.rsqrt(jnp.mean(v * v, axis=1, keepdims=True) + EPS) * gain


class Gather:
    def __init__(self, buf, slot, me, ssem, rsem):
        self.buf, self.slot, self.me = buf, slot, me
        self.ssem, self.rsem = ssem, rsem
        self.sent = []

    def place(self, h, i, j, core=None):
        x, y, z, c = self.me
        c = c if core is None else core
        if h == 0:
            return self.slot(mod4(x + i), mod4(y + j), c)
        return self.slot(mod4(x + j), mod4(y + i), c)

    def to(self, h, axis, step):
        x, y, z, c = self.me
        if (h == 0) == (axis == 0):
            return device(x + step, y, z, c)
        return device(x, y + step, z, c)

    def view(self, slot, h, cols):
        return self.buf.at[slot, pl.ds(80 * h, 80), cols]

    def send(self, h, i, j, cols, target, k):
        ref = self.view(self.place(h, i, j), h, cols)
        cp = rcopy(ref, ref, self.ssem.at[h, k], self.rsem.at[h, k], target)
        cp.start()
        self.sent.append(cp)

    def recv(self, h, i, j, cols, k, core=None):
        ref = self.view(self.place(h, i, j, core), h, cols)
        rcopy(ref, ref, self.ssem.at[h, k], self.rsem.at[h, k], self.to(h, 0, 1)).wait_recv()

    ALL = slice(0, WC)
    LEFT = slice(0, WC // 2)
    RIGHT = slice(WC // 2, WC)
    OFF = (0, -1, 1, 2)

    def sibling(self, h, ii, jj):
        x, y, z, c = self.me
        self.send(h, self.OFF[ii], self.OFF[jj], self.ALL, device(x, y, z, 1 - c), 20 + 4 * ii + jj)

    def first(self):
        for h in range(2):
            self.send(h, 0, 0, self.ALL, self.to(h, 0, 1), 0)
            self.send(h, 0, 0, self.ALL, self.to(h, 0, -1), 1)
        for h in range(2):
            self.second_send(h, 0)
            self.sibling(h, 0, 0)

    def first_recv(self):
        for h in range(2):
            self.recv(h, -1, 0, self.ALL, 0)
            self.send(h, -1, 0, self.LEFT, self.to(h, 0, 1), 2)
            self.recv(h, 1, 0, self.ALL, 1)
            self.send(h, 1, 0, self.RIGHT, self.to(h, 0, -1), 3)
        for h in range(2):
            self.second_send(h, 1)
            self.second_send(h, 2)
            self.sibling(h, 1, 0)
            self.sibling(h, 2, 0)

    def first_last(self):
        for h in range(2):
            self.recv(h, 2, 0, self.LEFT, 2)
            self.recv(h, 2, 0, self.RIGHT, 3)
            self.second_send(h, 3)
            self.sibling(h, 3, 0)

    def second_send(self, h, ii):
        i = self.OFF[ii]
        self.send(h, i, 0, self.ALL, self.to(h, 1, 1), 4 + 2 * ii)
        self.send(h, i, 0, self.ALL, self.to(h, 1, -1), 5 + 2 * ii)

    def second_recv(self, ii):
        i = self.OFF[ii]
        for h in range(2):
            self.recv(h, i, -1, self.ALL, 4 + 2 * ii)
            self.send(h, i, -1, self.LEFT, self.to(h, 1, 1), 12 + 2 * ii)
            self.recv(h, i, 1, self.ALL, 5 + 2 * ii)
            self.send(h, i, 1, self.RIGHT, self.to(h, 1, -1), 13 + 2 * ii)
            self.sibling(h, ii, 1)
            self.sibling(h, ii, 2)

    def second_last(self, ii):
        i = self.OFF[ii]
        for h in range(2):
            self.recv(h, i, 2, self.LEFT, 12 + 2 * ii)
            self.recv(h, i, 2, self.RIGHT, 13 + 2 * ii)
            self.sibling(h, ii, 3)

    def finish(self):
        c = self.me[3]
        for h in range(2):
            for ii in range(4):
                for jj in range(4):
                    self.recv(h, self.OFF[ii], self.OFF[jj], self.ALL, 20 + 4 * ii + jj, 1 - c)

    def drain(self):
        for cp in self.sent:
            cp.wait_send()
        self.sent = []


class Ring:
    def __init__(self, buf, slot, me, ssem, rsem, cols):
        self.buf, self.slot, self.me = buf, slot, me
        self.ssem, self.rsem = ssem, rsem
        self.cols = cols
        self.sent = []

    def view(self, origin, half):
        return self.buf.at[self.slot(lax.rem(origin + 16, 8)), pl.ds(160 * half, 160)]

    def send(self, way, half, k, src=None):
        x, y, z, c = self.me
        d = 0 if way > 0 else 1
        ref = self.view(z - way * (k - 1), half)
        cp = rcopy(ref if src is None else src, ref, self.ssem.at[d, half, k - 1],
                   self.rsem.at[d, half, k - 1], device(x, y, z + way, c))
        cp.start()
        self.sent.append(cp)

    def recv(self, way, half, k):
        x, y, z, c = self.me
        d = 0 if way > 0 else 1
        ref = self.view(z - way * k, half)
        rcopy(ref, ref, self.ssem.at[d, half, k - 1], self.rsem.at[d, half, k - 1],
              device(x, y, z + way, c)).wait_recv()
        if k < 3 or (k == 3 and (half == 0) == (way > 0)):
            self.send(way, half, k + 1)

    def drain(self):
        for cp in self.sent:
            cp.wait_send()
        self.sent = []


def mega(x_in, wq_in, wo_in, info_in, g0, g1, qg, kg, cos, sin, mask, lanes,
         land, info_land,
         XX, WQ, WO, A, ACC, HID, HB, PP, RSS, RSR, SS, SEND, VAL, INFO,
         own_sem, swap_s, swap_r, xs, xr, xcs, xcr, wqs, wqr, ts, tr, wos, wor,
         as_, ar, rss, rsr, sss, ssr, es, er, ns, nr):
    e = lax.axis_index("engine")
    t = lax.axis_index("tensor")
    x, y, a = e // 8, lax.rem(e, 4), lax.rem(e // 4, 2)
    zl, c = t // 2, lax.rem(t, 2)
    z = a * 4 + zl
    me = (x, y, z, c)
    sib = device(x, y, z, 1 - c)
    partner = device(x, y, z + 4, 1 - c)
    moved = a != c
    t_to = device(x, 2 * y + 1 + zl, a * 4 + y, c)
    t_from = device(x, zl, a * 4 + mod4(y - 2 * zl - 1), c)

    bar = pltpu.get_barrier_semaphore()
    for other in (device(x + 1, y, z, c), device(x - 1, y, z, c), device(x, y + 1, z, c),
                  device(x, y - 1, z, c), device(x, y, z + 1, c), device(x, y, z - 1, c),
                  sib, partner, t_to, t_from):
        pl.semaphore_signal(bar, inc=1, device_id=other, device_id_type=MESH)
    pl.semaphore_wait(bar, 10)

    def x_slot(origin):
        oa, ol = origin // 4, lax.rem(origin, 4)
        return jnp.where(oa == c, 2 * ol + c, 8 + ol)

    def wq_slot(sx, sy, sc):
        return sx * 8 + sc * 4 + sy

    def wo_slot(sx, sy, sc):
        return (2 * mod4(sy - 2 * zl - 1) + sc) * 4 + sx

    swap_slot = x * 8 + a * 4 + y

    def swap_copies():
        return (
            rcopy(wq_in, WQ.at[swap_slot], swap_s.at[0], swap_r.at[0], partner),
            rcopy(info_in, INFO, swap_s.at[1], swap_r.at[1], partner),
        )

    def stay_copies():
        return (
            pltpu.make_async_copy(wq_in, WQ.at[swap_slot], own_sem.at[0]),
            pltpu.make_async_copy(info_in, INFO, own_sem.at[1]),
        )

    @pl.when(moved)
    def _():
        for cp in swap_copies():
            cp.start()

    @pl.when(jnp.logical_not(moved))
    def _():
        for cp in stay_copies():
            cp.start()

    ring = Ring(XX, x_slot, me, xs, xr, 640)
    for way, half in ((1, 0), (-1, 1), (1, 1), (-1, 0)):
        ring.send(way, half, 1, x_in.at[pl.ds(160 * half, 160)])
    own_x = pltpu.make_async_copy(x_in, XX.at[x_slot(z)], own_sem.at[2])
    own_x.start()

    def x_cross(origin, half, src=None):
        origin = lax.rem(origin + 16, 8)
        oa, ol = origin // 4, lax.rem(origin, 4)

        @pl.when(oa != c)
        def _():
            rows = pl.ds(160 * half, 160)
            rcopy(XX.at[8 + ol, rows] if src is None else src, XX.at[2 * ol + c, rows],
                  xcs.at[ol, half], xcr.at[ol, half], sib).start()

    def x_recv(way, half, k):
        ring.recv(way, half, k)
        x_cross(z - way * k, half)

    for half in range(2):
        x_cross(z, half, x_in.at[pl.ds(160 * half, 160)])

    x_recv(1, 0, 1)
    x_recv(-1, 1, 1)

    @pl.when(moved)
    def _():
        for cp in swap_copies():
            cp.wait()

    @pl.when(jnp.logical_not(moved))
    def _():
        for cp in stay_copies():
            cp.wait()

    gq = Gather(WQ, wq_slot, me, wqs, wqr)
    gq.first()
    x_recv(1, 1, 1)
    x_recv(-1, 0, 1)
    gq.first_recv()
    x_recv(1, 0, 2)
    x_recv(-1, 1, 2)
    gq.first_last()
    gq.second_recv(0)
    x_recv(1, 1, 2)
    x_recv(-1, 0, 2)
    gq.second_recv(1)
    gq.second_recv(2)
    gq.second_last(0)
    x_recv(1, 0, 3)
    x_recv(-1, 1, 3)
    t_slot = (2 * zl + c) * 4 + x
    shift = rcopy(wo_in, WO.at[t_slot], ts, tr, t_to)
    shift.start()
    gq.second_recv(3)
    gq.second_last(1)
    x_recv(1, 1, 3)
    x_recv(-1, 0, 3)
    gq.second_last(2)
    gq.second_last(3)
    x_recv(1, 0, 4)
    x_recv(-1, 1, 4)
    shift.wait_send()
    t_mine = wo_slot(x, y, c)
    rcopy(wo_in, WO.at[t_mine], ts, tr, t_to).wait_recv()
    go = Gather(WO, wo_slot, me, wos, wor)
    go.first()
    gq.finish()
    own_x.wait()
    for ol in range(4):
        for half in range(2):
            rows = pl.ds(160 * half, 160)
            rcopy(XX.at[8 + ol, rows], XX.at[2 * ol + 1 - c, rows],
                  xcs.at[ol, half], xcr.at[ol, half], sib).wait_recv()

    ACC[...] = jnp.zeros_like(ACC)

    def qkv_step(i, total):
        xv = XX[i].astype(F32)
        total = total + jnp.sum(xv * xv, axis=1, keepdims=True)
        xn = (xv * g0[i]).astype(BF)
        w = WQ[pl.ds(4 * i, 4)].reshape(640, WC)
        ACC[...] += jnp.dot(xn, w, preferred_element_type=F32)
        return total

    total = lax.fori_loop(0, 8, qkv_step, jnp.zeros((TOK, 1), F32))
    r0 = lax.rsqrt(total / 5120.0 + EPS)
    go.first_recv()
    cosv, sinv = cos[...], sin[...]
    VAL[:, 0:128] = rope(head_norm(ACC[:, 512:640] * r0, kg[0:1]), cosv, sinv).astype(BF)
    VAL[:, 128:256] = (ACC[:, 640:768] * r0).astype(BF)
    for g in range(4):
        cols = slice(128 * g, 128 * g + 128)
        A[z, :, cols] = rope(head_norm(ACC[:, cols] * r0, qg[...]), cosv, sinv).astype(BF)
    go.first_last()
    for n in range(TOK // CB):
        rows = slice(CB * n, CB * n + CB)
        q = jnp.concatenate([A[z, rows, 128 * g:128 * g + 128] for g in range(4)], axis=0)
        s = lax.dot_general(q, VAL[rows, 0:128], NT, preferred_element_type=F32)
        w = jnp.where(mask[...] > 0, jnp.exp(s / jnp.sqrt(F32(128.0))), 0.0)
        p = (w / jnp.sum(w, axis=1, keepdims=True)).astype(BF)
        o = jnp.dot(p, VAL[rows, 128:256], preferred_element_type=F32).astype(BF)
        for g in range(4):
            A[z, rows, 128 * g:128 * g + 128] = o[CB * g:CB * g + CB]

    att = Ring(A, lambda origin: origin, me, as_, ar, 512)
    for way, half in ((1, 0), (-1, 1), (1, 1), (-1, 0)):
        att.send(way, half, 1)
    go.second_recv(0)

    def exchange_target(d):
        return (d, 2 * zl + a)

    mine = x * 8 + c * 4 + y

    def same(d):
        return jnp.logical_and(d == e, a == c)

    def list_step(d, carry):
        @pl.when(same(d))
        def _():
            pltpu.make_async_copy(INFO, info_land.at[mine], nr.at[mine]).start()

        @pl.when(jnp.logical_not(same(d)))
        def _():
            rcopy(INFO, info_land.at[mine], ns.at[d], nr.at[mine], exchange_target(d)).start()
        return carry

    pick_row = lax.broadcasted_iota(jnp.int32, (640, 160), 0)
    pick_col = lax.broadcasted_iota(jnp.int32, (640, 160), 1)
    pick = (pick_row == pick_col + 160 * zl).astype(BF)
    for sx in range(4):
        HID[sx] = jnp.dot(XX[2 * sx + a], pick, preferred_element_type=F32)

    def out_step(origin):
        origin = lax.rem(origin + 16, 8)
        head = 2 * lax.rem(origin, 4) + origin // 4

        def one(sx, carry):
            w = WO[head * 4 + sx, :, 0:512]
            part = lax.dot_general(A[origin], w, NT, preferred_element_type=F32)
            HID[sx] += part.astype(BF).astype(F32)
            return carry

        lax.fori_loop(0, 4, one, 0)

    att.recv(1, 0, 1)
    att.recv(-1, 1, 1)
    go.second_recv(1)
    att.recv(1, 1, 1)
    att.recv(-1, 0, 1)
    go.second_recv(2)
    go.second_last(0)
    att.recv(1, 0, 2)
    att.recv(-1, 1, 2)
    go.second_recv(3)
    go.second_last(1)
    att.recv(1, 1, 2)
    att.recv(-1, 0, 2)
    go.second_last(2)
    go.second_last(3)
    go.finish()
    out_step(z)
    out_step(z - 1)
    out_step(z + 1)
    att.recv(1, 0, 3)
    att.recv(-1, 1, 3)
    out_step(z - 2)
    out_step(z + 2)
    att.recv(1, 1, 3)
    att.recv(-1, 0, 3)
    lax.fori_loop(0, 32, list_step, 0)
    out_step(z - 3)
    out_step(z + 3)
    att.recv(1, 0, 4)
    att.recv(-1, 1, 4)
    out_step(z + 4)

    col = jnp.zeros((TOK, 1), F32)
    for sx in range(4):
        hv = HID[sx]
        col = col + jnp.sum(hv * hv, axis=1, keepdims=True)
        HB[sx] = (hv * g1[sx * 8 + a * 4 + zl]).astype(BF)
    eye = (lax.broadcasted_iota(jnp.int32, (TOK, TOK), 0)
           == lax.broadcasted_iota(jnp.int32, (TOK, TOK), 1))
    SS[z] = jnp.sum(jnp.where(eye, col, 0.0), axis=0, keepdims=True)
    ss_sent = []
    for k in range(1, 8):
        cp = rcopy(SS.at[z], SS.at[z], sss.at[k], ssr.at[k], device(x, y, z + k, c))
        cp.start()
        ss_sent.append(cp)

    def partial(dest):
        dest = lax.rem(dest + 16, 8)
        head = 2 * lax.rem(dest, 4) + dest // 4
        out = jnp.dot(HB[0], WO[head * 4, :, 512:768], preferred_element_type=F32)
        for sx in range(1, 4):
            out = out + jnp.dot(HB[sx], WO[head * 4 + sx, :, 512:768], preferred_element_type=F32)
        PP[dest] = out

    rs_sent = []

    def rs_send(way, half, s, value):
        d = 0 if way > 0 else 1
        RSS[d, half, s] = value.astype(BF)
        cp = rcopy(RSS.at[d, half, s], RSR.at[d, half, s], rss.at[d, half, s],
                   rsr.at[d, half, s], device(x, y, z + way, c))
        cp.start()
        rs_sent.append(cp)

    def rs_recv(way, half, s):
        d = 0 if way > 0 else 1
        rcopy(RSS.at[d, half, s], RSR.at[d, half, s], rss.at[d, half, s],
              rsr.at[d, half, s], device(x, y, z + way, c)).wait_recv()
        return RSR[d, half, s].astype(F32)

    def hops(way, half):
        return 4 if (half == 0) == (way > 0) else 3

    def own_part(way, half, s):
        dest = lax.rem(z + way * (hops(way, half) - s) + 16, 8)
        return PP[dest, pl.ds(160 * half, 160)]

    order = ((1, 0), (-1, 1), (1, 1), (-1, 0))
    partial(z + 4)
    rs_send(1, 0, 0, own_part(1, 0, 0))
    rs_send(-1, 1, 0, own_part(-1, 1, 0))
    partial(z + 3)
    rs_send(1, 1, 0, own_part(1, 1, 0))
    partial(z - 3)
    rs_send(-1, 0, 0, own_part(-1, 0, 0))
    partial(z + 2)
    partial(z - 2)
    partial(z + 1)
    partial(z - 1)
    partial(z)
    for s in range(3):
        for way, half in order:
            last = hops(way, half) - 1
            if s < last:
                rs_send(way, half, s + 1, rs_recv(way, half, s) + own_part(way, half, s + 1))
    ss_total = SS[z]
    for k in range(1, 8):
        origin = lax.rem(z - k + 16, 8)
        rcopy(SS.at[origin], SS.at[origin], sss.at[k], ssr.at[k], device(x, y, z + k, c)).wait_recv()
        ss_total = ss_total + SS[origin]
    r1 = lax.rsqrt(jnp.sum(jnp.where(eye, ss_total, 0.0), axis=1, keepdims=True) / 5120.0 + EPS)

    info = jnp.broadcast_to(INFO[...].astype(F32), (8, 128)).astype(BF)
    er_ = lax.broadcasted_iota(jnp.int32, (128, TOK), 0)
    row_of, tok_of = lanes[0:1, :], lanes[1:2, :]
    dest_l = jnp.dot(info, (er_ == row_of).astype(BF), preferred_element_type=F32)[0:1]
    len_l = jnp.dot(info, (er_ == row_of + 16).astype(BF), preferred_element_type=F32)[0:1]
    dest_l = dest_l.astype(jnp.int32)
    live = tok_of < len_l.astype(jnp.int32)
    key_a = jnp.where(jnp.logical_and(live, tok_of < 16), dest_l * 16 + tok_of, -1000)
    key_b = jnp.where(jnp.logical_and(live, tok_of >= 16), dest_l * 16 + tok_of - 16, -1000)
    place = lax.broadcasted_iota(jnp.int32, (512, TOK), 0)

    for half in range(2):
        way = 1 if half == 0 else -1
        rows = slice(160 * half, 160 * half + 160)
        kv = PP[z, rows] + rs_recv(way, half, 3) + rs_recv(-way, half, 2)
        kv = kv * r1[rows]
        VAL[rows, 256:384] = rope(head_norm(kv[:, 0:128], kg[1:2]), cos[rows], sin[rows]).astype(BF)
        VAL[rows, 384:512] = kv[:, 128:256].astype(BF)

    head_rows = jnp.dot((place == key_a).astype(BF), VAL[...], preferred_element_type=F32).astype(BF)
    SEND[:, :, 0:512] = head_rows.reshape(32, 16, 512)
    tail = jnp.zeros((512, 128), F32)
    for f in range(4):
        tail = tail + jnp.dot((place == key_b + 4 * f).astype(BF), VAL[:, 128 * f:128 * f + 128],
                              preferred_element_type=F32)
    SEND[:, :, 512:640] = tail.astype(BF).reshape(32, 16, 128)

    def send_step(d, carry):
        @pl.when(same(d))
        def _():
            pltpu.make_async_copy(SEND.at[d], land.at[mine], er.at[mine]).start()

        @pl.when(jnp.logical_not(same(d)))
        def _():
            rcopy(SEND.at[d], land.at[mine], es.at[d], er.at[mine], exchange_target(d)).start()
        return carry

    lax.fori_loop(0, 32, send_step, 0)

    def recv_step(s, carry):
        rcopy(SEND.at[s], land.at[s], es.at[s], er.at[s], exchange_target(s)).wait_recv()
        rcopy(INFO, info_land.at[s], ns.at[s], nr.at[s], exchange_target(s)).wait_recv()

        @pl.when(jnp.logical_not(same(s)))
        def _():
            rcopy(SEND.at[s], land.at[s], es.at[s], er.at[s], exchange_target(s)).wait_send()
            rcopy(INFO, info_land.at[s], ns.at[s], nr.at[s], exchange_target(s)).wait_send()
        return carry

    lax.fori_loop(0, 32, recv_step, 0)

    for part in (ring, gq, go, att):
        part.drain()
    for cp in ss_sent + rs_sent:
        cp.wait_send()
    for ol in range(4):
        @pl.when(c == 0)
        def _(ol=ol):
            for half in range(2):
                rows = pl.ds(160 * half, 160)
                rcopy(XX.at[8 + ol, rows], XX.at[2 * ol, rows], xcs.at[ol, half], xcr.at[ol, half], sib).wait_send()

        @pl.when(c == 1)
        def _(ol=ol):
            for half in range(2):
                rows = pl.ds(160 * half, 160)
                rcopy(XX.at[8 + ol, rows], XX.at[2 * ol + 1, rows], xcs.at[ol, half], xcr.at[ol, half], sib).wait_send()


def place_rows(land, key, out):
    at = lax.broadcasted_iota(jnp.int32, (512, 512), 0)
    pick = (at == key[...]).astype(BF)
    rows = jnp.dot(pick, land[...].reshape(512, 640), preferred_element_type=F32).astype(BF)
    rows = rows.reshape(32, 16, 640)
    for f in range(4):
        out[f, :, 0:16, :] = rows[:, :, 128 * f:128 * f + 128]
        out[f, :, 16:20, :] = rows[:, 4 * f:4 * f + 4, 512:640]


def tables():
    half = 64
    pos = (np.arange(TOK) % SPAN).astype(np.float32)
    freq = np.power(ROTARY_BASE, -np.arange(half, dtype=np.float64) * 2.0 / 128).astype(np.float32)
    angle = (pos[:, None] * freq[None, :]).astype(np.float32).astype(np.float64)
    cos, sin = np.cos(angle), np.sin(angle)
    cos = np.concatenate([cos, cos], axis=1).astype(np.float32)
    sin = np.concatenate([-sin, sin], axis=1).astype(np.float32)
    i, j = np.arange(CB)[:, None], np.arange(CB)[None, :]
    mask = ((i // SPAN == j // SPAN) & (j <= i)).astype(np.float32)
    mask = np.tile(mask, (4, 1))
    lanes = np.zeros((8, TOK), np.int32)
    lanes[0] = np.arange(TOK) // SPAN
    lanes[1] = np.arange(TOK) % SPAN
    return cos, sin, mask, lanes


def body(token_states, row_len, row_dest, norm_gain, q_gain, k_gain,
         q_weight, kv_weight0, out_weight, kv_weight1):
    x2 = token_states.reshape(TOK, 640)
    wq = jnp.concatenate([q_weight, kv_weight0.reshape(160, 256)], axis=1)
    wo = jnp.concatenate([out_weight, kv_weight1.reshape(160, 256)], axis=1)
    info = jnp.concatenate([row_dest, row_len, jnp.zeros((96,), jnp.int32)]).reshape(1, 128)
    g0 = norm_gain[0].reshape(8, 1, 640)
    g1 = norm_gain[1].reshape(32, 1, 160)
    cos, sin, mask, lanes = tables()
    vm = pl.BlockSpec(memory_space=pltpu.VMEM)
    hbm = pl.BlockSpec(memory_space=pl.ANY)
    dma = pltpu.SemaphoreType.DMA
    land, info_land = pl.pallas_call(
        mega,
        out_shape=(jax.ShapeDtypeStruct((32, 16, 640), BF),
                   jax.ShapeDtypeStruct((32, 1, 128), jnp.int32)),
        in_specs=[hbm, hbm, hbm, hbm] + [vm] * 8,
        out_specs=(vm, vm),
        scratch_shapes=[
            pltpu.VMEM((12, TOK, 640), BF),
            pltpu.VMEM((32, 160, WC), BF),
            pltpu.VMEM((32, 160, WC), BF),
            pltpu.VMEM((8, TOK, 512), BF),
            pltpu.VMEM((TOK, WC), F32),
            pltpu.VMEM((4, TOK, 160), F32),
            pltpu.VMEM((4, TOK, 160), BF),
            pltpu.VMEM((8, TOK, 256), F32),
            pltpu.VMEM((2, 2, 4, 160, 256), BF),
            pltpu.VMEM((2, 2, 4, 160, 256), BF),
            pltpu.VMEM((8, 1, TOK), F32),
            pltpu.VMEM((32, 16, 640), BF),
            pltpu.VMEM((TOK, 512), BF),
            pltpu.VMEM((1, 128), jnp.int32),
            dma((3,)), dma((2,)), dma((2,)),
            dma((2, 2, 4)), dma((2, 2, 4)), dma((4, 2)), dma((4, 2)),
            dma((2, 36)), dma((2, 36)), dma, dma, dma((2, 36)), dma((2, 36)),
            dma((2, 2, 4)), dma((2, 2, 4)), dma((2, 2, 4)), dma((2, 2, 4)),
            dma((8,)), dma((8,)), dma((32,)), dma((32,)), dma((32,)), dma((32,)),
        ],
        compiler_params=pltpu.CompilerParams(
            collective_id=0, has_side_effects=True, vmem_limit_bytes=56 * 2**20),
        name="prefill",
    )(x2, wq, wo, info, g0, g1, q_gain.reshape(1, 128), k_gain,
      jnp.asarray(cos), jnp.asarray(sin), jnp.asarray(mask), jnp.asarray(lanes))
    mine = lax.axis_index("engine")
    here = jnp.any(info_land[:, 0, :16] == mine, axis=1)
    slot = jnp.cumsum(here.astype(jnp.int32)) - 1
    key = jnp.where(here, slot * 16, -1000)[:, None] + jnp.arange(16, dtype=jnp.int32)[None, :]
    out = pl.pallas_call(
        place_rows,
        out_shape=jax.ShapeDtypeStruct((4, 32, SPAN, 128), BF),
        in_specs=[vm, vm],
        out_specs=vm,
        compiler_params=pltpu.CompilerParams(vmem_limit_bytes=32 * 2**20),
        name="place_rows",
    )(land, key.reshape(1, 512))
    return out.reshape(2, 2, 32, SPAN, 128)


def solution(mesh):
    in_specs = (
        P("engine", None, "tensor"), P("engine"), P("engine"), P(), P(), P(),
        P("engine", "tensor"), P("engine", None, "tensor"),
        P("engine", "tensor"), P("engine", None, "tensor"),
    )
    out_specs = P(None, None, "engine", None, "tensor")
    return jax.shard_map(body, mesh=mesh, in_specs=in_specs, out_specs=out_specs, check_vma=False)
```

```python
import functools

import jax
import jax.numpy as jnp
import numpy as np
from jax import lax
from jax.experimental import pallas as pl
from jax.experimental.pallas import tpu as pltpu
from jax.sharding import PartitionSpec as P

EPS = 1e-06
ROTARY_BASE = 1000000.0
MESH = pl.DeviceIdType.MESH
TOK = 320
SPAN = 20
WC = 768
CB = 80
F32 = jnp.float32
BF = jnp.bfloat16
NT = (((1,), (1,)), ((), ()))


def mod4(v):
    return lax.rem(v + 8, 4)


def device(x, y, z, c):
    z = lax.rem(z + 16, 8)
    return (mod4(x) * 8 + (z // 4) * 4 + mod4(y), lax.rem(z, 4) * 2 + c)


def rcopy(src, dst, send_sem, recv_sem, target):
    return pltpu.make_async_remote_copy(
        src_ref=src, dst_ref=dst, send_sem=send_sem, recv_sem=recv_sem,
        device_id=target, device_id_type=MESH,
    )


def rope(v, cos, sin):
    return v * cos + pltpu.roll(v, 64, 1) * sin


def head_norm(v, gain):
    return v * lax.rsqrt(jnp.mean(v * v, axis=1, keepdims=True) + EPS) * gain


class Gather:
    def __init__(self, buf, slot, me, ssem, rsem):
        self.buf, self.slot, self.me = buf, slot, me
        self.ssem, self.rsem = ssem, rsem
        self.sent = []

    def place(self, h, i, j, core=None):
        x, y, z, c = self.me
        c = c if core is None else core
        if h == 0:
            return self.slot(mod4(x + i), mod4(y + j), c)
        return self.slot(mod4(x + j), mod4(y + i), c)

    def to(self, h, axis, step):
        x, y, z, c = self.me
        if (h == 0) == (axis == 0):
            return device(x + step, y, z, c)
        return device(x, y + step, z, c)

    def view(self, slot, h, cols):
        return self.buf.at[slot, pl.ds(80 * h, 80), cols]

    def send(self, h, i, j, cols, target, k):
        ref = self.view(self.place(h, i, j), h, cols)
        cp = rcopy(ref, ref, self.ssem.at[h, k], self.rsem.at[h, k], target)
        cp.start()
        self.sent.append(cp)

    def recv(self, h, i, j, cols, k, core=None):
        ref = self.view(self.place(h, i, j, core), h, cols)
        rcopy(ref, ref, self.ssem.at[h, k], self.rsem.at[h, k], self.to(h, 0, 1)).wait_recv()

    ALL = slice(0, WC)
    LEFT = slice(0, WC // 2)
    RIGHT = slice(WC // 2, WC)
    OFF = (0, -1, 1, 2)

    def sibling(self, h, ii, jj):
        x, y, z, c = self.me
        self.send(h, self.OFF[ii], self.OFF[jj], self.ALL, device(x, y, z, 1 - c), 20 + 4 * ii + jj)

    def first(self):
        for h in range(2):
            self.send(h, 0, 0, self.ALL, self.to(h, 0, 1), 0)
            self.send(h, 0, 0, self.ALL, self.to(h, 0, -1), 1)
        for h in range(2):
            self.second_send(h, 0)
            self.sibling(h, 0, 0)

    def first_drain(self):
        for h in range(2):
            for k, cols in ((0, self.ALL), (1, self.ALL), (4, self.ALL), (5, self.ALL), (20, self.ALL)):
                ref = self.view(self.place(h, 0, 0), h, cols)
                rcopy(ref, ref, self.ssem.at[h, k], self.rsem.at[h, k], self.to(h, 0, 1)).wait_send()

    def first_recv(self):
        for h in range(2):
            self.recv(h, -1, 0, self.ALL, 0)
            self.send(h, -1, 0, self.LEFT, self.to(h, 0, 1), 2)
            self.recv(h, 1, 0, self.ALL, 1)
            self.send(h, 1, 0, self.RIGHT, self.to(h, 0, -1), 3)
        for h in range(2):
            self.second_send(h, 1)
            self.second_send(h, 2)
            self.sibling(h, 1, 0)
            self.sibling(h, 2, 0)

    def first_last(self):
        for h in range(2):
            self.recv(h, 2, 0, self.LEFT, 2)
            self.recv(h, 2, 0, self.RIGHT, 3)
            self.second_send(h, 3)
            self.sibling(h, 3, 0)

    def second_send(self, h, ii):
        i = self.OFF[ii]
        self.send(h, i, 0, self.ALL, self.to(h, 1, 1), 4 + 2 * ii)
        self.send(h, i, 0, self.ALL, self.to(h, 1, -1), 5 + 2 * ii)

    def second_recv(self, ii):
        i = self.OFF[ii]
        for h in range(2):
            self.recv(h, i, -1, self.ALL, 4 + 2 * ii)
            self.send(h, i, -1, self.LEFT, self.to(h, 1, 1), 12 + 2 * ii)
            self.recv(h, i, 1, self.ALL, 5 + 2 * ii)
            self.send(h, i, 1, self.RIGHT, self.to(h, 1, -1), 13 + 2 * ii)
            self.sibling(h, ii, 1)
            self.sibling(h, ii, 2)

    def second_last(self, ii):
        i = self.OFF[ii]
        for h in range(2):
            self.recv(h, i, 2, self.LEFT, 12 + 2 * ii)
            self.recv(h, i, 2, self.RIGHT, 13 + 2 * ii)
            self.sibling(h, ii, 3)

    def finish(self):
        c = self.me[3]
        for h in range(2):
            for ii in range(4):
                for jj in range(4):
                    self.recv(h, self.OFF[ii], self.OFF[jj], self.ALL, 20 + 4 * ii + jj, 1 - c)

    def drain(self):
        for cp in self.sent:
            cp.wait_send()
        self.sent = []


class Ring:
    LONG = {1: (0, 1), -1: (2, 3)}

    def __init__(self, buf, slot, me, ssem, rsem):
        self.buf, self.slot, self.me = buf, slot, me
        self.ssem, self.rsem = ssem, rsem
        self.sent = []

    def order(self, k):
        lo, sh = self.LONG[1], self.LONG[-1]
        if k == 4:
            return ((1, lo[0]), (-1, sh[0]), (1, lo[1]), (-1, sh[1]))
        return ((1, lo[0]), (-1, sh[0]), (1, sh[0]), (-1, lo[0]),
                (1, lo[1]), (-1, sh[1]), (1, sh[1]), (-1, lo[1]))

    def view(self, origin, part):
        return self.buf.at[self.slot(lax.rem(origin + 16, 8)), pl.ds(80 * part, 80)]

    def send(self, way, part, k, src=None):
        x, y, z, c = self.me
        d = 0 if way > 0 else 1
        ref = self.view(z - way * (k - 1), part)
        cp = rcopy(ref if src is None else src, ref, self.ssem.at[d, part, k - 1],
                   self.rsem.at[d, part, k - 1], device(x, y, z + way, c))
        cp.start()
        self.sent.append(cp)

    def recv(self, way, part, k):
        x, y, z, c = self.me
        d = 0 if way > 0 else 1
        ref = self.view(z - way * k, part)
        rcopy(ref, ref, self.ssem.at[d, part, k - 1], self.rsem.at[d, part, k - 1],
              device(x, y, z + way, c)).wait_recv()
        if k < 3 or (k == 3 and part in self.LONG[way]):
            self.send(way, part, k + 1)

    def drain(self):
        for cp in self.sent:
            cp.wait_send()
        self.sent = []


def mega(tok_in, q_in, kv0_in, out_in, kv1_in, dest_in, len_in, gains_in, qg_in, kg_in,
         cos_in, sin_in, mask_in, lanes_in, caches,
         XS, KV0, KV1, DEST, LEN, gains, qg, kg, cos, sin, mask, lanes, land0, land1, info_land, OUT,
         WQS, WOS, XX, WQ, WO, A, ACC, HID, HB, PP, RSS, RSR, SS, SEND0, SEND1, VAL, INFO, MY,
         in_sem, own_sem, out_sem, swap_s, swap_r, xs, xr, xcs, xcr, wqs, wqr, ts, tr, wos, wor,
         as_, ar, rss, rsr, sss, ssr, es, er, fs, fr, ns, nr):
    e = lax.axis_index("engine")
    t = lax.axis_index("tensor")
    x, y, a = e // 8, lax.rem(e, 4), lax.rem(e // 4, 2)
    zl, c = t // 2, lax.rem(t, 2)
    z = a * 4 + zl
    me = (x, y, z, c)
    sib = device(x, y, z, 1 - c)
    partner = device(x, y, z + 4, 1 - c)
    moved = a != c

    def t_to(u):
        return device(x, zl + 1, a * 4 + 2 * u + lax.rem(y, 2), c)

    def t_from(yhi):
        return device(x, 2 * yhi + lax.rem(zl, 2), a * 4 + mod4(y - 1), c)

    bar = pltpu.get_barrier_semaphore()
    for other in (device(x + 1, y, z, c), device(x - 1, y, z, c), device(x, y + 1, z, c),
                  device(x, y - 1, z, c), device(x, y, z + 1, c), device(x, y, z - 1, c),
                  sib, partner, t_to(0), t_to(1), t_from(0), t_from(1)):
        pl.semaphore_signal(bar, inc=1, device_id=other, device_id_type=MESH)

    fetch = {}
    for n, (src, dst) in enumerate((
            (tok_in, XS), (kv0_in, KV0), (dest_in, DEST), (len_in, LEN), (kv1_in, KV1),
            (gains_in, gains), (qg_in, qg), (kg_in, kg), (cos_in, cos), (sin_in, sin),
            (mask_in, mask), (lanes_in, lanes))):
        fetch[n] = pltpu.make_async_copy(src, dst, in_sem.at[n])
        fetch[n].start()
    q_copy = pltpu.make_async_copy(q_in, WQS.at[:, pl.ds(0, 512)], own_sem.at[0])
    out_copy = pltpu.make_async_copy(out_in, WOS.at[:, pl.ds(0, 512)], own_sem.at[1])
    q_copy.start()
    out_copy.start()
    for n in (1, 2, 3):
        fetch[n].wait()
    for kind in range(2):
        WQS[:, 512 + 128 * kind:640 + 128 * kind] = KV0[:, kind, :]
    MY[...] = jnp.zeros_like(MY)
    MY[:, 0:16] = DEST[...]
    MY[:, 16:32] = LEN[...]
    q_copy.wait()
    fetch[0].wait()
    pl.semaphore_wait(bar, 12)

    def x_slot(origin):
        oa, ol = origin // 4, lax.rem(origin, 4)
        return jnp.where(oa == c, 2 * ol + c, 8 + ol)

    def wq_slot(sx, sy, sc):
        return sx * 8 + sc * 4 + sy

    def wo_slot(sx, sy, sc):
        return (2 * mod4(sy - 1) + sc) * 4 + sx

    swap_slot = x * 8 + a * 4 + y

    def swap_copies():
        return (
            rcopy(WQS, WQ.at[swap_slot], swap_s.at[0], swap_r.at[0], partner),
            rcopy(MY, INFO, swap_s.at[1], swap_r.at[1], partner),
        )

    def stay_copies():
        return (
            pltpu.make_async_copy(WQS, WQ.at[swap_slot], swap_r.at[0]),
            pltpu.make_async_copy(MY, INFO, swap_r.at[1]),
        )

    gq = Gather(WQ, wq_slot, me, wqs, wqr)
    ring = Ring(XX, x_slot, me, xs, xr)

    @pl.when(moved)
    def _():
        for cp in swap_copies():
            cp.start()

    @pl.when(jnp.logical_not(moved))
    def _():
        for cp in stay_copies():
            cp.start()

    for way, part in ring.order(1):
        ring.send(way, part, 1, XS.at[pl.ds(80 * part, 80)])
    own_x = pltpu.make_async_copy(XS, XX.at[x_slot(z)], own_sem.at[2])
    own_x.start()

    @pl.when(jnp.logical_not(moved))
    def _():
        for cp in stay_copies():
            cp.wait()
        gq.first()

    gq.sent = []
    def x_cross(origin, part, src=None):
        origin = lax.rem(origin + 16, 8)
        oa, ol = origin // 4, lax.rem(origin, 4)

        @pl.when(oa != c)
        def _():
            rows = pl.ds(80 * part, 80)
            rcopy(XX.at[8 + ol, rows] if src is None else src, XX.at[2 * ol + c, rows],
                  xcs.at[ol, part], xcr.at[ol, part], sib).start()

    def x_crossed(ol):
        for part in range(4):
            rows = pl.ds(80 * part, 80)
            rcopy(XX.at[8 + ol, rows], XX.at[2 * ol + 1 - c, rows],
                  xcs.at[ol, part], xcr.at[ol, part], sib).wait_recv()

    def x_recv(k, low=0, high=8):
        for way, part in ring.order(k)[low:high]:
            ring.recv(way, part, k)
            x_cross(z - way * k, part)

    for part in range(4):
        x_cross(z, part, XS.at[pl.ds(80 * part, 80)])

    fetch[4].wait()
    for kind in range(2):
        WOS[:, 512 + 128 * kind:640 + 128 * kind] = KV1[:, kind, :]
    x_recv(1, 0, 4)

    @pl.when(moved)
    def _():
        for cp in swap_copies():
            cp.wait()
        gq.first()

    gq.sent = []
    x_recv(1, 4, 8)
    x_recv(2, 0, 4)
    gq.first_recv()
    x_recv(2, 4, 8)
    out_copy.wait()

    def shift(u):
        return rcopy(WOS.at[pl.ds(80 * u, 80)],
                     WO.at[(2 * zl + c) * 4 + x, pl.ds(80 * (y // 2), 80)],
                     ts.at[u], tr.at[y // 2], t_to(u))

    for u in range(2):
        shift(u).start()
    gq.first_last()
    gq.second_recv(0)
    x_recv(3, 0, 4)
    gq.second_recv(1)
    gq.second_recv(2)
    gq.second_last(0)
    x_recv(3, 4, 8)
    gq.second_recv(3)
    gq.second_last(1)
    for yhi in range(2):
        half = WO.at[wo_slot(x, y, c), pl.ds(80 * yhi, 80)]
        rcopy(half, half, ts.at[yhi], tr.at[yhi], sib).wait_recv()
    go = Gather(WO, wo_slot, me, wos, wor)
    go.first()
    gq.second_last(2)
    gq.second_last(3)
    gq.finish()
    own_x.wait()

    for n in range(5, 12):
        fetch[n].wait()

    ACC[...] = jnp.zeros_like(ACC)

    def qkv_step(i, total):
        xv = XX[i].astype(F32)
        total = total + jnp.sum(xv * xv, axis=1, keepdims=True)
        xn = (xv * gains[0:1, pl.ds(pl.multiple_of(640 * i, 128), 640)]).astype(BF)
        w = WQ[pl.ds(4 * i, 4)].reshape(640, WC)
        ACC[...] += jnp.dot(xn, w, preferred_element_type=F32)
        return total

    for n in range(1, 4):
        x_crossed(lax.rem(zl + n, 4))
    total = lax.fori_loop(
        0, 6, lambda j, s: qkv_step(2 * lax.rem(zl + 1 + j // 2, 4) + lax.rem(j, 2), s),
        jnp.zeros((TOK, 1), F32))
    x_recv(4, 0, 4)
    go.first_recv()
    x_crossed(zl)
    total = lax.fori_loop(0, 2, lambda j, s: qkv_step(2 * zl + j, s), total)
    r0 = lax.rsqrt(total / 5120.0 + EPS)
    cosv, sinv = cos[...], sin[...]
    VAL[:, 0:128] = rope(head_norm(ACC[:, 512:640] * r0, kg[0:1]), cosv, sinv).astype(BF)
    VAL[:, 128:256] = (ACC[:, 640:768] * r0).astype(BF)
    for g in range(4):
        cols = slice(128 * g, 128 * g + 128)
        A[z, :, cols] = rope(head_norm(ACC[:, cols] * r0, qg[...]), cosv, sinv).astype(BF)
    go.first_last()
    att = Ring(A, lambda origin: origin, me, as_, ar)
    for n in (0, 2, 1, 3):
        rows = slice(CB * n, CB * n + CB)
        keys = slice(0, CB * n + CB)
        q = jnp.concatenate([A[z, rows, 128 * g:128 * g + 128] for g in range(4)], axis=0)
        s = lax.dot_general(q, VAL[keys, 0:128], NT, preferred_element_type=F32)
        seen = jnp.concatenate([mask[rows, keys]] * 4, axis=0)
        w = jnp.where(seen > 0, jnp.exp(s / jnp.sqrt(F32(128.0))), 0.0)
        p = (w / jnp.sum(w, axis=1, keepdims=True)).astype(BF)
        o = jnp.dot(p, VAL[keys, 128:256], preferred_element_type=F32).astype(BF)
        for g in range(4):
            A[z, rows, 128 * g:128 * g + 128] = o[CB * g:CB * g + CB]
        att.send(1, n, 1)
        att.send(-1, n, 1)

    def att_recv(k, low=0, high=8):
        for way, part in att.order(k)[low:high]:
            att.recv(way, part, k)

    go.second_recv(0)

    info = jnp.broadcast_to(INFO[...].astype(F32), (8, 128)).astype(BF)
    lane = lax.broadcasted_iota(jnp.int32, (128, TOK), 0)
    row_of, tok_of = lanes[0:1, :], lanes[1:2, :]
    dest_l = jnp.dot(info, (lane == row_of).astype(BF), preferred_element_type=F32)[0:1]
    len_l = jnp.dot(info, (lane == row_of + 16).astype(BF), preferred_element_type=F32)[0:1]
    dest_l = dest_l.astype(jnp.int32)
    live = tok_of < len_l.astype(jnp.int32)
    key_a = jnp.where(jnp.logical_and(live, tok_of < 16), dest_l * 16 + tok_of, -1000)
    key_b = jnp.where(jnp.logical_and(live, tok_of >= 16), dest_l * 16 + tok_of - 16, -1000)
    place = lax.broadcasted_iota(jnp.int32, (512, TOK), 0)

    def head_rows(cols):
        return jnp.dot((place == key_a).astype(BF), VAL[:, cols], preferred_element_type=F32)

    def tail_rows(f):
        return jnp.dot((place == key_b + 4 * f).astype(BF), VAL[:, 128 * f:128 * f + 128],
                       preferred_element_type=F32)

    SEND0[...] = head_rows(slice(0, 256)).astype(BF).reshape(32, 16, 256)
    tail = tail_rows(0) + tail_rows(1)
    SEND1[:, :, 256:384] = tail.astype(BF).reshape(32, 16, 128)

    pick_row = lax.broadcasted_iota(jnp.int32, (640, 160), 0)
    pick_col = lax.broadcasted_iota(jnp.int32, (640, 160), 1)
    u, v = zl // 2, lax.rem(zl, 2)
    pick = pick_row == pick_col + jnp.where(pick_col >= 80, 240, 0) + (160 * v + 80 * u)
    pick_b, pick_f = pick.astype(BF), pick.astype(F32)
    g1 = []
    for sx in range(4):
        HID[sx] = jnp.dot(XX[2 * sx + a], pick_b, preferred_element_type=F32)
        at = 1280 * sx
        gv = jnp.where(a == 0, gains[1:2, at:at + 640], gains[1:2, at + 640:at + 1280])
        g1.append(jnp.dot(jnp.broadcast_to(gv, (8, 640)), pick_f, preferred_element_type=F32,
                          precision=lax.Precision.HIGHEST)[0:1])

    mine = x * 8 + c * 4 + y

    def target(d):
        return (d, 2 * zl + a)

    def same(d):
        return jnp.logical_and(d == e, a == c)

    def hand_out(srcs):
        def step(d, carry):
            @pl.when(same(d))
            def _():
                for src, dst, ss, rs in srcs(d):
                    pltpu.make_async_copy(src, dst, rs.at[mine]).start()

            @pl.when(jnp.logical_not(same(d)))
            def _():
                for src, dst, ss, rs in srcs(d):
                    rcopy(src, dst, ss.at[d], rs.at[mine], target(d)).start()
            return carry

        lax.fori_loop(0, 32, step, 0)

    def early(d):
        return ((INFO, info_land.at[mine], ns, nr), (SEND0.at[d], land0.at[mine], es, er))

    def late(d):
        return ((SEND1.at[d], land1.at[mine], fs, fr),)

    def out_step(origin):
        origin = lax.rem(origin + 16, 8)
        head = 2 * lax.rem(origin, 4) + origin // 4
        for sx in range(4):
            part = lax.dot_general(A[origin], WO[head * 4 + sx, :, 0:512], NT,
                                   preferred_element_type=F32)
            HID[sx] += part.astype(BF).astype(F32)

    att_recv(1)
    go.second_recv(1)
    go.second_recv(2)
    att_recv(2, 0, 4)
    go.second_last(0)
    go.second_recv(3)
    att_recv(2, 4, 8)
    go.second_last(1)
    go.second_last(2)
    att_recv(3, 0, 4)
    go.second_last(3)
    att_recv(3, 4, 8)
    go.finish()
    hand_out(early)
    for k in (0, -1, 1, -2, 2, -3, 3):
        out_step(z + k)
    att_recv(4, 0, 4)
    out_step(z + 4)

    col = jnp.zeros((TOK, 1), F32)
    for sx in range(4):
        hv = HID[sx]
        col = col + jnp.sum(hv * hv, axis=1, keepdims=True)
        HB[sx] = (hv * g1[sx]).astype(BF)

    def partial(dest):
        dest = lax.rem(dest + 16, 8)
        head = 2 * lax.rem(dest, 4) + dest // 4
        out = jnp.dot(HB[0], WO[head * 4, :, 512:768], preferred_element_type=F32)
        for sx in range(1, 4):
            out = out + jnp.dot(HB[sx], WO[head * 4 + sx, :, 512:768], preferred_element_type=F32)
        PP[dest] = out

    rs_sent = []

    def rs_copy(way, part, s):
        d = 0 if way > 0 else 1
        return rcopy(RSS.at[d, part, s], RSR.at[d, part, s], rss.at[d, part, s],
                     rsr.at[d, part, s], device(x, y, z + way, c))

    def rs_send(way, part, s, value):
        RSS[0 if way > 0 else 1, part, s] = value.astype(BF)
        cp = rs_copy(way, part, s)
        cp.start()
        rs_sent.append(cp)

    def rs_recv(way, part, s):
        rs_copy(way, part, s).wait_recv()
        return RSR[0 if way > 0 else 1, part, s].astype(F32)

    def hops(way, part):
        return 4 if part in Ring.LONG[way] else 3

    def own_part(way, part, s):
        dest = lax.rem(z + way * (hops(way, part) - s) + 16, 8)
        return PP[dest, pl.ds(80 * part, 80)]

    partial(z + 4)
    for way, part in ((1, 0), (-1, 2), (1, 1), (-1, 3)):
        rs_send(way, part, 0, own_part(way, part, 0))
    partial(z + 3)
    partial(z - 3)
    for way, part in ((1, 2), (-1, 0), (1, 3), (-1, 1)):
        rs_send(way, part, 0, own_part(way, part, 0))
    eye = (lax.broadcasted_iota(jnp.int32, (TOK, TOK), 0)
           == lax.broadcasted_iota(jnp.int32, (TOK, TOK), 1))
    SS[z] = jnp.sum(jnp.where(eye, col, 0.0), axis=0, keepdims=True)
    ss_sent = []
    for k in range(1, 8):
        cp = rcopy(SS.at[z], SS.at[z], sss.at[k], ssr.at[k], device(x, y, z + k, c))
        cp.start()
        ss_sent.append(cp)
    for k in (2, -2, 1, -1, 0):
        partial(z + k)
    ring_order = ((1, 0), (-1, 2), (1, 1), (-1, 3), (1, 2), (-1, 0), (1, 3), (-1, 1))
    for s in range(3):
        for way, part in ring_order:
            if s < hops(way, part) - 1:
                rs_send(way, part, s + 1, rs_recv(way, part, s) + own_part(way, part, s + 1))
    ss_total = SS[z]
    for k in range(1, 8):
        origin = lax.rem(z - k + 16, 8)
        rcopy(SS.at[origin], SS.at[origin], sss.at[k], ssr.at[k], device(x, y, z + k, c)).wait_recv()
        ss_total = ss_total + SS[origin]
    r1 = lax.rsqrt(jnp.sum(jnp.where(eye, ss_total, 0.0), axis=1, keepdims=True) / 5120.0 + EPS)

    for part in range(4):
        way = 1 if part in Ring.LONG[1] else -1
        rows = slice(80 * part, 80 * part + 80)
        kv = PP[z, rows] + rs_recv(-way, part, 2) + rs_recv(way, part, 3)
        kv = kv * r1[rows]
        VAL[rows, 256:384] = rope(head_norm(kv[:, 0:128], kg[1:2]), cos[rows], sin[rows]).astype(BF)
        VAL[rows, 384:512] = kv[:, 128:256].astype(BF)

    SEND1[:, :, 0:256] = head_rows(slice(256, 512)).astype(BF).reshape(32, 16, 256)
    tail = tail + tail_rows(2) + tail_rows(3)
    SEND1[:, :, 256:384] = tail.astype(BF).reshape(32, 16, 128)
    hand_out(late)

    def landed(srcs, dsts):
        def step(d, carry):
            for (src, _, ss, rs), dst in zip(srcs(d), dsts):
                rcopy(src, dst.at[d], ss.at[d], rs.at[d], target(d)).wait_recv()

            @pl.when(jnp.logical_not(same(d)))
            def _():
                for (src, _, ss, rs), dst in zip(srcs(d), dsts):
                    rcopy(src, dst.at[d], ss.at[d], rs.at[d], target(d)).wait_send()
            return carry

        lax.fori_loop(0, 32, step, 0)

    for part in (ring, gq, go, att):
        part.drain()
    for cp in ss_sent + rs_sent:
        cp.wait_send()
    for u in range(2):
        shift(u).wait_send()
    gq.first_drain()
    for ol in range(4):
        for part in range(4):
            rows = pl.ds(80 * part, 80)
            rcopy(XX.at[8 + ol, rows], XX.at[2 * ol + c, rows],
                  xcs.at[ol, part], xcr.at[ol, part], sib).wait_send()

    landed(early, (info_land, land0))
    lane = lax.broadcasted_iota(jnp.int32, (32, 128), 1)
    hit = jnp.logical_and(info_land[...].reshape(32, 128) == e, lane < 16)
    here = jnp.max(hit.astype(F32), axis=1, keepdims=True)
    before = (lax.broadcasted_iota(jnp.int32, (32, 32), 1)
              < lax.broadcasted_iota(jnp.int32, (32, 32), 0)).astype(BF)
    rank = jnp.dot(before, jnp.broadcast_to(here, (32, 128)).astype(BF), preferred_element_type=F32)
    key = jnp.where(here > 0, rank[:, 0:1], -1000.0)
    key = jnp.broadcast_to(key[:, None, :], (32, 16, 512))
    row = lax.broadcasted_iota(jnp.int32, (32, 16, 512), 1).astype(F32) * 32.0
    at = lax.broadcasted_iota(jnp.int32, (32, 16, 512), 2).astype(F32)
    pick_rows = (key + row == at).astype(BF).reshape(512, 512)
    tn = (((0,), (0,)), ((), ()))

    def settle(block):
        out = lax.dot_general(pick_rows, block, tn, preferred_element_type=F32)
        return out.astype(BF).reshape(16, 32, block.shape[1])

    rows0 = settle(land0[...].reshape(512, 256))
    for f in range(2):
        OUT[f, 0:16] = rows0[:, :, 128 * f:128 * f + 128]
    landed(late, (land1,))
    rows1 = settle(land1[...].reshape(512, 384))
    for f in range(2):
        OUT[2 + f, 0:16] = rows1[:, :, 128 * f:128 * f + 128]
    for f in range(4):
        OUT[f, 16:20] = rows1[4 * f:4 * f + 4, :, 256:384]
    put = pltpu.make_async_copy(OUT, caches, out_sem)
    put.start()
    put.wait()


def tables():
    half = 64
    where = np.arange(TOK) // 16
    pos = where.astype(np.float32)
    freq = np.power(ROTARY_BASE, -np.arange(half, dtype=np.float64) * 2.0 / 128).astype(np.float32)
    angle = (pos[:, None] * freq[None, :]).astype(np.float32).astype(np.float64)
    cos, sin = np.cos(angle), np.sin(angle)
    cos = np.concatenate([cos, cos], axis=1).astype(np.float32)
    sin = np.concatenate([-sin, sin], axis=1).astype(np.float32)
    i, j = np.arange(TOK)[:, None], np.arange(TOK)[None, :]
    mask = ((i % 16 == j % 16) & (j <= i)).astype(np.float32)
    lanes = np.zeros((8, TOK), np.int32)
    lanes[0] = np.arange(TOK) % 16
    lanes[1] = where
    return cos, sin, mask, lanes


def body(token_states, row_len, row_dest, norm_gain, q_gain, k_gain,
         q_weight, kv_weight0, out_weight, kv_weight1):
    cos, sin, mask, lanes = tables()
    hbm = pl.BlockSpec(memory_space=pl.ANY)
    dma = pltpu.SemaphoreType.DMA
    vmem = pltpu.VMEM
    out = pl.pallas_call(
        mega,
        out_shape=jax.ShapeDtypeStruct((4, SPAN, 32, 128), BF),
        in_specs=[hbm] * 14,
        out_specs=hbm,
        scratch_shapes=[
            vmem((TOK, 640), BF), vmem((160, 2, 128), BF), vmem((160, 2, 128), BF),
            vmem((1, 16), jnp.int32), vmem((1, 16), jnp.int32),
            vmem((2, 5120), F32), vmem((1, 128), F32), vmem((2, 128), F32),
            vmem((TOK, 128), F32), vmem((TOK, 128), F32), vmem((TOK, TOK), F32), vmem((8, TOK), jnp.int32),
            vmem((32, 16, 256), BF), vmem((32, 16, 384), BF), vmem((32, 1, 128), jnp.int32),
            vmem((4, SPAN, 32, 128), BF),
            vmem((160, WC), BF), vmem((160, WC), BF),
            vmem((12, TOK, 640), BF), vmem((32, 160, WC), BF), vmem((32, 160, WC), BF),
            vmem((8, TOK, 512), BF), vmem((TOK, WC), F32),
            vmem((4, TOK, 160), F32), vmem((4, TOK, 160), BF), vmem((8, TOK, 256), F32),
            vmem((2, 4, 4, 80, 256), BF), vmem((2, 4, 4, 80, 256), BF), vmem((8, 1, TOK), F32),
            vmem((32, 16, 256), BF), vmem((32, 16, 384), BF), vmem((TOK, 512), BF),
            vmem((1, 128), jnp.int32), vmem((1, 128), jnp.int32),
            dma((12,)), dma((3,)), dma, dma((2,)), dma((2,)),
            dma((2, 4, 4)), dma((2, 4, 4)), dma((4, 4)), dma((4, 4)),
            dma((2, 36)), dma((2, 36)), dma((2,)), dma((2,)), dma((2, 36)), dma((2, 36)),
            dma((2, 4, 4)), dma((2, 4, 4)), dma((2, 4, 4)), dma((2, 4, 4)),
            dma((8,)), dma((8,)), dma((32,)), dma((32,)), dma((32,)), dma((32,)),
            dma((32,)), dma((32,)),
        ],
        compiler_params=pltpu.CompilerParams(
            collective_id=0, has_side_effects=True, vmem_limit_bytes=58 * 2**20),
        name="prefill",
    )(token_states.transpose(1, 0, 2).reshape(TOK, 640), q_weight, kv_weight0, out_weight, kv_weight1,
      row_dest.reshape(1, 16), row_len.reshape(1, 16),
      norm_gain, q_gain.reshape(1, 128), k_gain,
      jnp.asarray(cos), jnp.asarray(sin), jnp.asarray(mask), jnp.asarray(lanes))
    return out.reshape(2, 2, SPAN, 32, 128).transpose(0, 1, 3, 2, 4)


def solution(mesh):
    in_specs = (
        P("engine", None, "tensor"), P("engine"), P("engine"), P(), P(), P(),
        P("engine", "tensor"), P("engine", None, "tensor"),
        P("engine", "tensor"), P("engine", None, "tensor"),
    )
    out_specs = P(None, None, "engine", None, "tensor")
    return jax.shard_map(body, mesh=mesh, in_specs=in_specs, out_specs=out_specs, check_vma=False)
```

```python
import functools

import jax
import jax.numpy as jnp
import numpy as np
from jax import lax
from jax.experimental import pallas as pl
from jax.experimental.pallas import tpu as pltpu
from jax.sharding import PartitionSpec as P

EPS = 1e-06
ROTARY_BASE = 1000000.0
MESH = pl.DeviceIdType.MESH
TOK = 320
SPAN = 20
WC = 768
CB = 80
F32 = jnp.float32
BF = jnp.bfloat16
NT = (((1,), (1,)), ((), ()))


def mod4(v):
    return lax.rem(v + 8, 4)


def device(x, y, z, c):
    z = lax.rem(z + 16, 8)
    return (mod4(x) * 8 + (z // 4) * 4 + mod4(y), lax.rem(z, 4) * 2 + c)


def rcopy(src, dst, send_sem, recv_sem, target):
    return pltpu.make_async_remote_copy(
        src_ref=src, dst_ref=dst, send_sem=send_sem, recv_sem=recv_sem,
        device_id=target, device_id_type=MESH,
    )


def rope(v, cos, sin):
    return v * cos + pltpu.roll(v, 64, 1) * sin


def head_norm(v, gain):
    return v * lax.rsqrt(jnp.mean(v * v, axis=1, keepdims=True) + EPS) * gain


class Gather:
    def __init__(self, buf, slot, me, ssem, rsem, csem):
        self.buf, self.slot, self.me = buf, slot, me
        self.ssem, self.rsem, self.csem = ssem, rsem, csem

    def place(self, h, i, j, core=None):
        x, y, z, c = self.me
        c = c if core is None else core
        if h == 0:
            return self.slot(mod4(x + i), mod4(y + j), c)
        return self.slot(mod4(x + j), mod4(y + i), c)

    def to(self, h, axis, step):
        x, y, z, c = self.me
        if (h == 0) == (axis == 0):
            return device(x + step, y, z, c)
        return device(x, y + step, z, c)

    def view(self, slot, h, cols):
        return self.buf.at[slot, pl.ds(80 * h, 80), cols]

    def send(self, h, i, j, cols, target, k):
        ref = self.view(self.place(h, i, j), h, cols)
        arrive = self.rsem.at[h, k] if k < 20 else self.csem
        rcopy(ref, ref, self.ssem, arrive, target).start()

    def recv(self, h, i, j, cols, k):
        ref = self.view(self.place(h, i, j), h, cols)
        rcopy(ref, ref, self.ssem, self.rsem.at[h, k], self.to(h, 0, 1)).wait_recv()

    ALL = slice(0, WC)
    LEFT = slice(0, WC // 2)
    RIGHT = slice(WC // 2, WC)
    OFF = (0, -1, 1, 2)

    def sibling(self, h, ii, jj):
        x, y, z, c = self.me
        self.send(h, self.OFF[ii], self.OFF[jj], self.ALL, device(x, y, z, 1 - c), 20 + 4 * ii + jj)

    def first(self):
        for h in range(2):
            self.send(h, 0, 0, self.ALL, self.to(h, 0, 1), 0)
            self.send(h, 0, 0, self.ALL, self.to(h, 0, -1), 1)
        for h in range(2):
            self.second_send(h, 0)
            self.sibling(h, 0, 0)

    def first_recv(self):
        for h in range(2):
            self.recv(h, -1, 0, self.ALL, 0)
            self.send(h, -1, 0, self.LEFT, self.to(h, 0, 1), 2)
            self.recv(h, 1, 0, self.ALL, 1)
            self.send(h, 1, 0, self.RIGHT, self.to(h, 0, -1), 3)
        for h in range(2):
            self.second_send(h, 1)
            self.second_send(h, 2)
            self.sibling(h, 1, 0)
            self.sibling(h, 2, 0)

    def first_last(self):
        for h in range(2):
            self.recv(h, 2, 0, self.LEFT, 2)
            self.recv(h, 2, 0, self.RIGHT, 3)
            self.second_send(h, 3)
            self.sibling(h, 3, 0)

    def second_send(self, h, ii):
        i = self.OFF[ii]
        self.send(h, i, 0, self.ALL, self.to(h, 1, 1), 4 + 2 * ii)
        self.send(h, i, 0, self.ALL, self.to(h, 1, -1), 5 + 2 * ii)

    def second_recv(self, ii):
        i = self.OFF[ii]
        for h in range(2):
            self.recv(h, i, -1, self.ALL, 4 + 2 * ii)
            self.send(h, i, -1, self.LEFT, self.to(h, 1, 1), 12 + 2 * ii)
            self.recv(h, i, 1, self.ALL, 5 + 2 * ii)
            self.send(h, i, 1, self.RIGHT, self.to(h, 1, -1), 13 + 2 * ii)
            self.sibling(h, ii, 1)
            self.sibling(h, ii, 2)

    def second_last(self, ii):
        i = self.OFF[ii]
        for h in range(2):
            self.recv(h, i, 2, self.LEFT, 12 + 2 * ii)
            self.recv(h, i, 2, self.RIGHT, 13 + 2 * ii)
            self.sibling(h, ii, 3)

    def whole(self, blocks):
        x, y, z, c = self.me
        ref = self.buf.at[pl.ds(0, blocks)]
        return rcopy(ref, ref, self.ssem, self.csem, device(x, y, z, 1 - c))

    def finish(self):
        self.whole(16).wait_recv()

    def drain(self):
        self.whole(31).wait_send()


class Ring:
    LONG = {1: (0, 1), -1: (2, 3)}

    def __init__(self, buf, slot, me, ssem, rsem):
        self.buf, self.slot, self.me = buf, slot, me
        self.ssem, self.rsem = ssem, rsem

    def order(self, k):
        lo, sh = self.LONG[1], self.LONG[-1]
        if k == 4:
            return ((1, lo[0]), (-1, sh[0]), (1, lo[1]), (-1, sh[1]))
        return ((1, lo[0]), (-1, sh[0]), (1, sh[0]), (-1, lo[0]),
                (1, lo[1]), (-1, sh[1]), (1, sh[1]), (-1, lo[1]))

    def view(self, origin, part):
        return self.buf.at[self.slot(lax.rem(origin + 16, 8)), pl.ds(80 * part, 80)]

    def send(self, way, part, k, src=None):
        x, y, z, c = self.me
        d = 0 if way > 0 else 1
        ref = self.view(z - way * (k - 1), part)
        rcopy(ref if src is None else src, ref, self.ssem,
              self.rsem.at[d, part, k - 1], device(x, y, z + way, c)).start()

    def recv(self, way, part, k):
        x, y, z, c = self.me
        d = 0 if way > 0 else 1
        ref = self.view(z - way * k, part)
        rcopy(ref, ref, self.ssem, self.rsem.at[d, part, k - 1],
              device(x, y, z + way, c)).wait_recv()
        if k < 3 or (k == 3 and part in self.LONG[way]):
            self.send(way, part, k + 1)

    def drain(self):
        x, y, z, c = self.me
        ref = self.buf.at[pl.ds(0, 7)]
        rcopy(ref, ref, self.ssem, self.rsem.at[0, 0, 0], device(x, y, z + 1, c)).wait_send()


def mega(tok_in, q_in, kv0_in, out_in, kv1_in, dest_in, len_in, gains_in, qg_in, kg_in,
         cos_in, sin_in, mask_in, lanes_in, caches,
         XS, KV0, KV1, DEST, LEN, gains, qg, kg, cos, sin, mask, lanes, land0, land1, info_land, OUT,
         WQS, WOS, XX, WQ, WO, A, ACC, HID, HB, PP, RSS, RSR, SS, SEND0, SEND1, VAL, INFO, MY,
         in_sem, own_sem, out_sem, swap_s, swap_r, xs, xr, xcs, xcr, wqs, wqr, wqc, ts, tr, wos, wor, woc,
         as_, ar, rss, rsr, sss, ssr, es, er, fs, fr, ns, nr):
    e = lax.axis_index("engine")
    t = lax.axis_index("tensor")
    x, y, a = e // 8, lax.rem(e, 4), lax.rem(e // 4, 2)
    zl, c = t // 2, lax.rem(t, 2)
    z = a * 4 + zl
    me = (x, y, z, c)
    sib = device(x, y, z, 1 - c)
    partner = device(x, y, z + 4, 1 - c)
    moved = a != c

    def t_to(u):
        return device(x, zl + 1, a * 4 + 2 * u + lax.rem(y, 2), c)

    def t_from(yhi):
        return device(x, 2 * yhi + lax.rem(zl, 2), a * 4 + mod4(y - 1), c)

    bar = pltpu.get_barrier_semaphore()
    for other in (device(x + 1, y, z, c), device(x - 1, y, z, c), device(x, y + 1, z, c),
                  device(x, y - 1, z, c), device(x, y, z + 1, c), device(x, y, z - 1, c),
                  sib, partner, t_to(0), t_to(1), t_from(0), t_from(1)):
        pl.semaphore_signal(bar, inc=1, device_id=other, device_id_type=MESH)

    def x_slot(origin):
        oa, ol = origin // 4, lax.rem(origin, 4)
        return jnp.where(oa == c, 2 * ol + c, 8 + ol)

    ring = Ring(XX, x_slot, me, xs, xr)
    own_x = pltpu.make_async_copy(XS, XX.at[x_slot(z)], own_sem.at[2])

    def x_first():
        for way, part in ring.order(1):
            ring.send(way, part, 1, XS.at[pl.ds(80 * part, 80)])
        own_x.start()

    fetch = {}
    for n, (src, dst) in enumerate((
            (tok_in, XS), (kv0_in, KV0), (dest_in, DEST), (len_in, LEN), (kv1_in, KV1),
            (gains_in, gains), (qg_in, qg), (kg_in, kg), (cos_in, cos), (sin_in, sin),
            (mask_in, mask), (lanes_in, lanes))):
        fetch[n] = pltpu.make_async_copy(src, dst, in_sem.at[n])
        fetch[n].start()
    q_copy = pltpu.make_async_copy(q_in, WQS.at[:, pl.ds(0, 512)], own_sem.at[0])
    out_copy = pltpu.make_async_copy(out_in, WOS.at[:, pl.ds(0, 512)], own_sem.at[1])
    q_copy.start()
    out_copy.start()
    for n in (1, 2, 3):
        fetch[n].wait()
    for kind in range(2):
        WQS[:, 512 + 128 * kind:640 + 128 * kind] = KV0[:, kind, :]
    MY[...] = jnp.zeros_like(MY)
    MY[:, 0:16] = DEST[...]
    MY[:, 16:32] = LEN[...]
    q_copy.wait()
    fetch[0].wait()
    pl.semaphore_wait(bar, 12)

    def wq_slot(sx, sy, sc):
        return sx * 8 + sc * 4 + sy

    def wo_slot(sx, sy, sc):
        return (2 * mod4(sy - 1) + sc) * 4 + sx

    swap_slot = x * 8 + a * 4 + y

    def swap_copies():
        return (
            rcopy(WQS, WQ.at[swap_slot], swap_s.at[0], swap_r.at[0], partner),
            rcopy(MY, INFO, swap_s.at[1], swap_r.at[1], partner),
        )

    def stay_copies():
        return (
            pltpu.make_async_copy(WQS, WQ.at[swap_slot], swap_r.at[0]),
            pltpu.make_async_copy(MY, INFO, swap_r.at[1]),
        )

    gq = Gather(WQ, wq_slot, me, wqs, wqr, wqc)

    @pl.when(moved)
    def _():
        for cp in swap_copies():
            cp.start()

    @pl.when(jnp.logical_not(moved))
    def _():
        for cp in stay_copies():
            cp.start()

    x_first()

    @pl.when(jnp.logical_not(moved))
    def _():
        for cp in stay_copies():
            cp.wait()
        gq.first()

    def x_cross(origin, part, src=None):
        origin = lax.rem(origin + 16, 8)
        oa, ol = origin // 4, lax.rem(origin, 4)

        @pl.when(oa != c)
        def _():
            rows = pl.ds(80 * part, 80)
            rcopy(XX.at[8 + ol, rows] if src is None else src, XX.at[2 * ol + c, rows],
                  xcs, xcr.at[ol], sib).start()

    def x_crossed(ol):
        rcopy(XX.at[8 + ol], XX.at[2 * ol + 1 - c], xcs, xcr.at[ol], sib).wait_recv()

    def x_recv(k, low=0, high=8):
        for way, part in ring.order(k)[low:high]:
            ring.recv(way, part, k)
            x_cross(z - way * k, part)

    for part in range(4):
        x_cross(z, part, XS.at[pl.ds(80 * part, 80)])

    fetch[4].wait()
    for kind in range(2):
        WOS[:, 512 + 128 * kind:640 + 128 * kind] = KV1[:, kind, :]
    def moved_first():
        @pl.when(moved)
        def _():
            for cp in swap_copies():
                cp.wait()
            gq.first()


    def shift(u):
        return rcopy(WOS.at[pl.ds(80 * u, 80)],
                     WO.at[(2 * zl + c) * 4 + x, pl.ds(80 * (y // 2), 80)],
                     ts, tr.at[y // 2], t_to(u))

    def shift_start():
        out_copy.wait()
        for u in range(2):
            shift(u).start()

    def shift_recv():
        for yhi in range(2):
            half = WO.at[wo_slot(x, y, c), pl.ds(80 * yhi, 80)]
            rcopy(half, half, ts, tr.at[yhi], sib).wait_recv()

    go = Gather(WO, wo_slot, me, wos, wor, woc)
    moved_first()
    x_recv(1, 0, 4)
    gq.first_recv()
    x_recv(1, 4, 8)
    gq.first_last()
    x_recv(2, 0, 4)
    gq.second_recv(0)
    gq.second_recv(1)
    x_recv(2, 4, 8)
    shift_start()
    gq.second_recv(2)
    gq.second_last(0)
    x_recv(3, 0, 4)
    gq.second_recv(3)
    gq.second_last(1)
    gq.second_last(2)
    x_recv(3, 4, 8)
    gq.second_last(3)
    shift_recv()
    go.first()
    gq.finish()
    own_x.wait()
    for n in range(5, 12):
        fetch[n].wait()

    ACC[...] = jnp.zeros_like(ACC)

    def qkv_step(i, total):
        xv = XX[i].astype(F32)
        total = total + jnp.sum(xv * xv, axis=1, keepdims=True)
        xn = (xv * gains[0:1, pl.ds(pl.multiple_of(640 * i, 128), 640)]).astype(BF)
        w = WQ[pl.ds(4 * i, 4)].reshape(640, WC)
        ACC[...] += jnp.dot(xn, w, preferred_element_type=F32)
        return total

    for n in range(1, 4):
        x_crossed(lax.rem(zl + n, 4))
    total = jnp.zeros((TOK, 1), F32)

    def some(low, high, total):
        return lax.fori_loop(
            low, high, lambda j, s: qkv_step(2 * lax.rem(zl + 1 + j // 2, 4) + lax.rem(j, 2), s), total)

    total = some(0, 6, total)
    x_recv(4, 0, 4)
    go.first_recv()
    x_crossed(zl)
    total = some(6, 8, total)
    r0 = lax.rsqrt(total / 5120.0 + EPS)
    cosv, sinv = cos[...], sin[...]
    VAL[:, 0:128] = rope(head_norm(ACC[:, 512:640] * r0, kg[0:1]), cosv, sinv).astype(BF)
    VAL[:, 128:256] = (ACC[:, 640:768] * r0).astype(BF)
    for g in range(4):
        cols = slice(128 * g, 128 * g + 128)
        A[z, :, cols] = rope(head_norm(ACC[:, cols] * r0, qg[...]), cosv, sinv).astype(BF)
    go.first_last()
    att = Ring(A, lambda origin: origin, me, as_, ar)
    for n in (0, 2, 1, 3):
        rows = slice(CB * n, CB * n + CB)
        keys = slice(0, CB * n + CB)
        q = jnp.concatenate([A[z, rows, 128 * g:128 * g + 128] for g in range(4)], axis=0)
        s = lax.dot_general(q, VAL[keys, 0:128], NT, preferred_element_type=F32)
        seen = jnp.concatenate([mask[rows, keys]] * 4, axis=0)
        w = jnp.where(seen > 0, jnp.exp(s / jnp.sqrt(F32(128.0))), 0.0)
        p = (w / jnp.sum(w, axis=1, keepdims=True)).astype(BF)
        o = jnp.dot(p, VAL[keys, 128:256], preferred_element_type=F32).astype(BF)
        for g in range(4):
            A[z, rows, 128 * g:128 * g + 128] = o[CB * g:CB * g + CB]
        att.send(1, n, 1)
        att.send(-1, n, 1)

    def att_recv(k, low=0, high=8):
        for way, part in att.order(k)[low:high]:
            att.recv(way, part, k)

    def go_second_recv_0():
        go.second_recv(0)

    info = jnp.broadcast_to(INFO[...].astype(F32), (8, 128)).astype(BF)
    lane = lax.broadcasted_iota(jnp.int32, (128, TOK), 0)
    row_of, tok_of = lanes[0:1, :], lanes[1:2, :]
    dest_l = jnp.dot(info, (lane == row_of).astype(BF), preferred_element_type=F32)[0:1]
    len_l = jnp.dot(info, (lane == row_of + 16).astype(BF), preferred_element_type=F32)[0:1]
    dest_l = dest_l.astype(jnp.int32)
    live = tok_of < len_l.astype(jnp.int32)
    key_a = jnp.where(jnp.logical_and(live, tok_of < 16), dest_l * 16 + tok_of, -1000)
    key_b = jnp.where(jnp.logical_and(live, tok_of >= 16), dest_l * 16 + tok_of - 16, -1000)
    place = lax.broadcasted_iota(jnp.int32, (512, TOK), 0)

    def head_rows(cols):
        return jnp.dot((place == key_a).astype(BF), VAL[:, cols], preferred_element_type=F32)

    def tail_rows(f):
        return jnp.dot((place == key_b + 4 * f).astype(BF), VAL[:, 128 * f:128 * f + 128],
                       preferred_element_type=F32)

    g1, tails = [], []

    def prep():
        SEND0[...] = head_rows(slice(0, 256)).astype(BF).reshape(32, 16, 256)
        tail = tail_rows(0) + tail_rows(1)
        SEND1[:, :, 256:384] = tail.astype(BF).reshape(32, 16, 128)
        tails.append(tail)
        pick_row = lax.broadcasted_iota(jnp.int32, (640, 160), 0)
        pick_col = lax.broadcasted_iota(jnp.int32, (640, 160), 1)
        u, v = zl // 2, lax.rem(zl, 2)
        pick = pick_row == pick_col + jnp.where(pick_col >= 80, 240, 0) + (160 * v + 80 * u)
        pick_b, pick_f = pick.astype(BF), pick.astype(F32)
        for sx in range(4):
            HID[sx] = jnp.dot(XX[2 * sx + a], pick_b, preferred_element_type=F32)
            at = 1280 * sx
            gv = jnp.where(a == 0, gains[1:2, at:at + 640], gains[1:2, at + 640:at + 1280])
            g1.append(jnp.dot(jnp.broadcast_to(gv, (8, 640)), pick_f, preferred_element_type=F32,
                              precision=lax.Precision.HIGHEST)[0:1])

    mine = x * 8 + c * 4 + y

    def target(d):
        return (d, 2 * zl + a)

    def same(d):
        return jnp.logical_and(d == e, a == c)

    def hand_out(srcs):
        def step(d, carry):

            @pl.when(same(d))
            def _():
                for src, dst, ss, rs in srcs(d):
                    pltpu.make_async_copy(src, dst, rs).start()

            @pl.when(jnp.logical_not(same(d)))
            def _():
                for src, dst, ss, rs in srcs(d):
                    rcopy(src, dst, ss, rs, target(d)).start()
            return carry

        lax.fori_loop(0, 32, step, 0)

    def early(d):
        return ((INFO, info_land.at[mine], ns, nr), (SEND0.at[d], land0.at[mine], es, er))

    def late(d):
        return ((SEND1.at[d], land1.at[mine], fs, fr),)

    def out_step(origin):
        origin = lax.rem(origin + 16, 8)
        head = 2 * lax.rem(origin, 4) + origin // 4
        for sx in range(4):
            part = lax.dot_general(A[origin], WO[head * 4 + sx, :, 0:512], NT,
                                   preferred_element_type=F32)
            HID[sx] += part.astype(BF).astype(F32)

    go_second_recv_0()
    att_recv(1, 0, 2)
    go.second_recv(1)
    att_recv(1, 2, 8)
    go.second_recv(2)
    prep()
    att_recv(2, 0, 2)
    go.second_last(0)
    att_recv(2, 2, 4)
    go.second_recv(3)
    att_recv(2, 4, 8)
    go.second_last(1)
    go.second_last(2)
    att_recv(3, 0, 2)
    go.second_last(3)
    att_recv(3, 2, 8)
    go.finish()
    for k in (0, -1, 1, -2, 2, -3, 3):
        out_step(z + k)
    hand_out(early)
    att_recv(4, 0, 4)
    out_step(z + 4)


    col = jnp.zeros((TOK, 1), F32)
    for sx in range(4):
        hv = HID[sx]
        col = col + jnp.sum(hv * hv, axis=1, keepdims=True)
        HB[sx] = (hv * g1[sx]).astype(BF)

    def partial(dest):
        dest = lax.rem(dest + 16, 8)
        head = 2 * lax.rem(dest, 4) + dest // 4
        out = jnp.dot(HB[0], WO[head * 4, :, 512:768], preferred_element_type=F32)
        for sx in range(1, 4):
            out = out + jnp.dot(HB[sx], WO[head * 4 + sx, :, 512:768], preferred_element_type=F32)
        PP[dest] = out

    def rs_at(way, part, s):
        d = 0 if way > 0 else 14
        long = Ring.LONG[way]
        return d + (4 * long.index(part) + s if part in long else 8 + 3 * Ring.LONG[-way].index(part) + s)

    def rs_copy(way, part, s):
        n = rs_at(way, part, s)
        return rcopy(RSS.at[n], RSR.at[n], rss, rsr.at[n], device(x, y, z + way, c))

    def rs_send(way, part, s, value):
        RSS[rs_at(way, part, s)] = value.astype(BF)
        rs_copy(way, part, s).start()

    def rs_recv(way, part, s):
        rs_copy(way, part, s).wait_recv()
        return RSR[rs_at(way, part, s)].astype(F32)

    def hops(way, part):
        return 4 if part in Ring.LONG[way] else 3

    def own_part(way, part, s):
        dest = lax.rem(z + way * (hops(way, part) - s) + 16, 8)
        return PP[dest, pl.ds(80 * part, 80)]

    partial(z + 4)
    for way, part in ((1, 0), (-1, 2), (1, 1), (-1, 3)):
        rs_send(way, part, 0, own_part(way, part, 0))
    partial(z + 3)
    partial(z - 3)
    for way, part in ((1, 2), (-1, 0), (1, 3), (-1, 1)):
        rs_send(way, part, 0, own_part(way, part, 0))
    eye = (lax.broadcasted_iota(jnp.int32, (TOK, TOK), 0)
           == lax.broadcasted_iota(jnp.int32, (TOK, TOK), 1))
    SS[z] = jnp.sum(jnp.where(eye, col, 0.0), axis=0, keepdims=True)
    for k in range(1, 8):
        rcopy(SS.at[z], SS.at[z], sss, ssr, device(x, y, z + k, c)).start()
    for k in (2, -2, 1, -1, 0):
        partial(z + k)
    ring_order = ((1, 0), (-1, 2), (1, 1), (-1, 3), (1, 2), (-1, 0), (1, 3), (-1, 1))
    for s in range(3):
        for way, part in ring_order:
            if s < hops(way, part) - 1:
                rs_send(way, part, s + 1, rs_recv(way, part, s) + own_part(way, part, s + 1))
    rcopy(SS.at[pl.ds(0, 7)], SS.at[pl.ds(0, 7)], sss, ssr, sib).wait_recv()
    ss_total = SS[0]
    for k in range(1, 8):
        ss_total = ss_total + SS[k]
    r1 = lax.rsqrt(jnp.sum(jnp.where(eye, ss_total, 0.0), axis=1, keepdims=True) / 5120.0 + EPS)

    for part in range(4):
        way = 1 if part in Ring.LONG[1] else -1
        rows = slice(80 * part, 80 * part + 80)
        kv = PP[z, rows] + rs_recv(-way, part, 2) + rs_recv(way, part, 3)
        kv = kv * r1[rows]
        VAL[rows, 256:384] = rope(head_norm(kv[:, 0:128], kg[1:2]), cos[rows], sin[rows]).astype(BF)
        VAL[rows, 384:512] = kv[:, 128:256].astype(BF)

    SEND1[:, :, 0:256] = head_rows(slice(256, 512)).astype(BF).reshape(32, 16, 256)
    tail = tails[0] + tail_rows(2) + tail_rows(3)
    SEND1[:, :, 256:384] = tail.astype(BF).reshape(32, 16, 128)
    hand_out(late)

    def landed(groups):
        for dst, ss, rs in groups:
            rcopy(dst, dst, ss, rs, sib).wait_recv()

            @pl.when(a == c)
            def _(dst=dst, ss=ss, rs=rs):
                most = dst.at[pl.ds(0, 31)]
                rcopy(most, most, ss, rs, sib).wait_send()

            @pl.when(a != c)
            def _(dst=dst, ss=ss, rs=rs):
                rcopy(dst, dst, ss, rs, sib).wait_send()

    for part in (ring, gq, go, att):
        part.drain()
    rcopy(RSS, RSS, rss, rsr.at[0], sib).wait_send()
    rcopy(SS.at[pl.ds(0, 7)], SS.at[pl.ds(0, 7)], sss, ssr, sib).wait_send()
    rcopy(WOS, WOS, ts, tr.at[0], sib).wait_send()
    rcopy(XX.at[pl.ds(0, 4)], XX.at[pl.ds(0, 4)], xcs, xcr.at[0], sib).wait_send()

    landed(((info_land, ns, nr), (land0, es, er)))
    lane = lax.broadcasted_iota(jnp.int32, (32, 128), 1)
    hit = jnp.logical_and(info_land[...].reshape(32, 128) == e, lane < 16)
    here = jnp.max(hit.astype(F32), axis=1, keepdims=True)
    before = (lax.broadcasted_iota(jnp.int32, (32, 32), 1)
              < lax.broadcasted_iota(jnp.int32, (32, 32), 0)).astype(BF)
    rank = jnp.dot(before, jnp.broadcast_to(here, (32, 128)).astype(BF), preferred_element_type=F32)
    key = jnp.where(here > 0, rank[:, 0:1], -1000.0)
    key = jnp.broadcast_to(key[:, None, :], (32, 16, 512))
    row = lax.broadcasted_iota(jnp.int32, (32, 16, 512), 1).astype(F32) * 32.0
    at = lax.broadcasted_iota(jnp.int32, (32, 16, 512), 2).astype(F32)
    pick_rows = (key + row == at).astype(BF).reshape(512, 512)
    tn = (((0,), (0,)), ((), ()))

    def settle(block):
        out = lax.dot_general(pick_rows, block, tn, preferred_element_type=F32)
        return out.astype(BF).reshape(16, 32, block.shape[1])

    rows0 = settle(land0[...].reshape(512, 256))
    for f in range(2):
        OUT[f, 0:16] = rows0[:, :, 128 * f:128 * f + 128]
    landed(((land1, fs, fr),))
    rows1 = settle(land1[...].reshape(512, 384))
    for f in range(2):
        OUT[2 + f, 0:16] = rows1[:, :, 128 * f:128 * f + 128]
    for f in range(4):
        OUT[f, 16:20] = rows1[4 * f:4 * f + 4, :, 256:384]
    put = pltpu.make_async_copy(OUT, caches, out_sem)
    put.start()
    put.wait()


def tables():
    half = 64
    where = np.arange(TOK) // 16
    pos = where.astype(np.float32)
    freq = np.power(ROTARY_BASE, -np.arange(half, dtype=np.float64) * 2.0 / 128).astype(np.float32)
    angle = (pos[:, None] * freq[None, :]).astype(np.float32).astype(np.float64)
    cos, sin = np.cos(angle), np.sin(angle)
    cos = np.concatenate([cos, cos], axis=1).astype(np.float32)
    sin = np.concatenate([-sin, sin], axis=1).astype(np.float32)
    i, j = np.arange(TOK)[:, None], np.arange(TOK)[None, :]
    mask = ((i % 16 == j % 16) & (j <= i)).astype(np.float32)
    lanes = np.zeros((8, TOK), np.int32)
    lanes[0] = np.arange(TOK) % 16
    lanes[1] = where
    return cos, sin, mask, lanes


def body(token_states, row_len, row_dest, norm_gain, q_gain, k_gain,
         q_weight, kv_weight0, out_weight, kv_weight1):
    cos, sin, mask, lanes = tables()
    hbm = pl.BlockSpec(memory_space=pl.ANY)
    dma = pltpu.SemaphoreType.DMA
    vmem = pltpu.VMEM
    out = pl.pallas_call(
        mega,
        out_shape=jax.ShapeDtypeStruct((4, SPAN, 32, 128), BF),
        in_specs=[hbm] * 14,
        out_specs=hbm,
        scratch_shapes=[
            vmem((TOK, 640), BF), vmem((160, 2, 128), BF), vmem((160, 2, 128), BF),
            vmem((1, 16), jnp.int32), vmem((1, 16), jnp.int32),
            vmem((2, 5120), F32), vmem((1, 128), F32), vmem((2, 128), F32),
            vmem((TOK, 128), F32), vmem((TOK, 128), F32), vmem((TOK, TOK), F32), vmem((8, TOK), jnp.int32),
            vmem((32, 16, 256), BF), vmem((32, 16, 384), BF), vmem((32, 1, 128), jnp.int32),
            vmem((4, SPAN, 32, 128), BF),
            vmem((160, WC), BF), vmem((160, WC), BF),
            vmem((12, TOK, 640), BF), vmem((32, 160, WC), BF), vmem((32, 160, WC), BF),
            vmem((8, TOK, 512), BF), vmem((TOK, WC), F32),
            vmem((4, TOK, 160), F32), vmem((4, TOK, 160), BF), vmem((8, TOK, 256), F32),
            vmem((28, 80, 256), BF), vmem((28, 80, 256), BF), vmem((8, 1, TOK), F32),
            vmem((32, 16, 256), BF), vmem((32, 16, 384), BF), vmem((TOK, 512), BF),
            vmem((1, 128), jnp.int32), vmem((1, 128), jnp.int32),
            dma((12,)), dma((3,)), dma, dma((2,)), dma((2,)),
            dma, dma((2, 4, 4)), dma, dma((4,)),
            dma, dma((2, 20)), dma, dma, dma((2,)), dma, dma((2, 20)), dma,
            dma, dma((2, 4, 4)), dma, dma((28,)),
            dma, dma, dma, dma, dma, dma, dma, dma,
        ],
        compiler_params=pltpu.CompilerParams(
            collective_id=0, has_side_effects=True, vmem_limit_bytes=58 * 2**20),
        name="prefill",
    )(token_states.transpose(1, 0, 2).reshape(TOK, 640), q_weight, kv_weight0, out_weight, kv_weight1,
      row_dest.reshape(1, 16), row_len.reshape(1, 16),
      norm_gain, q_gain.reshape(1, 128), k_gain,
      jnp.asarray(cos), jnp.asarray(sin), jnp.asarray(mask), jnp.asarray(lanes))
    return out.reshape(2, 2, SPAN, 32, 128).transpose(0, 1, 3, 2, 4)


def solution(mesh):
    in_specs = (
        P("engine", None, "tensor"), P("engine"), P("engine"), P(), P(), P(),
        P("engine", "tensor"), P("engine", None, "tensor"),
        P("engine", "tensor"), P("engine", None, "tensor"),
    )
    out_specs = P(None, None, "engine", None, "tensor")
    return jax.shard_map(body, mesh=mesh, in_specs=in_specs, out_specs=out_specs, check_vma=False)
```

```python
import functools

import jax
import jax.numpy as jnp
import numpy as np
from jax import lax
from jax.experimental import pallas as pl
from jax.experimental.pallas import tpu as pltpu
from jax.sharding import PartitionSpec as P

EPS = 1e-06
ROTARY_BASE = 1000000.0
MESH = pl.DeviceIdType.MESH
TOK = 320
SPAN = 20
WC = 768
CB = 80
F32 = jnp.float32
BF = jnp.bfloat16
NT = (((1,), (1,)), ((), ()))


def mod4(v):
    return lax.rem(v + 8, 4)


def device(x, y, z, c):
    z = lax.rem(z + 16, 8)
    return (mod4(x) * 8 + (z // 4) * 4 + mod4(y), lax.rem(z, 4) * 2 + c)


def rcopy(src, dst, send_sem, recv_sem, target):
    return pltpu.make_async_remote_copy(
        src_ref=src, dst_ref=dst, send_sem=send_sem, recv_sem=recv_sem,
        device_id=target, device_id_type=MESH,
    )


def rope(v, cos, sin):
    return v * cos + pltpu.roll(v, 64, 1) * sin


def head_norm(v, gain):
    return v * lax.rsqrt(jnp.mean(v * v, axis=1, keepdims=True) + EPS) * gain


class Gather:
    def __init__(self, buf, slot, me, ssem, rsem, csem):
        self.buf, self.slot, self.me = buf, slot, me
        self.ssem, self.rsem, self.csem = ssem, rsem, csem

    def place(self, h, i, j, core=None):
        x, y, z, c = self.me
        c = c if core is None else core
        if h == 0:
            return self.slot(mod4(x + i), mod4(y + j), c)
        return self.slot(mod4(x + j), mod4(y + i), c)

    def to(self, h, axis, step):
        x, y, z, c = self.me
        if (h == 0) == (axis == 0):
            return device(x + step, y, z, c)
        return device(x, y + step, z, c)

    def view(self, slot, h, cols):
        return self.buf.at[slot, pl.ds(80 * h, 80), cols]

    def send(self, h, i, j, cols, target, k):
        ref = self.view(self.place(h, i, j), h, cols)
        arrive = self.rsem.at[h, k] if k < 20 else self.csem
        rcopy(ref, ref, self.ssem, arrive, target).start()

    def recv(self, h, i, j, cols, k):
        ref = self.view(self.place(h, i, j), h, cols)
        rcopy(ref, ref, self.ssem, self.rsem.at[h, k], self.to(h, 0, 1)).wait_recv()

    ALL = slice(0, WC)
    LEFT = slice(0, WC // 2)
    RIGHT = slice(WC // 2, WC)
    OFF = (0, -1, 1, 2)

    def sibling(self, h, ii, jj):
        x, y, z, c = self.me
        self.send(h, self.OFF[ii], self.OFF[jj], self.ALL, device(x, y, z, 1 - c), 20 + 4 * ii + jj)

    def first(self):
        for h in range(2):
            self.send(h, 0, 0, self.ALL, self.to(h, 0, 1), 0)
            self.send(h, 0, 0, self.ALL, self.to(h, 0, -1), 1)
        for h in range(2):
            self.second_send(h, 0)
            self.sibling(h, 0, 0)

    def first_recv(self):
        for h in range(2):
            self.recv(h, -1, 0, self.ALL, 0)
            self.send(h, -1, 0, self.LEFT, self.to(h, 0, 1), 2)
            self.recv(h, 1, 0, self.ALL, 1)
            self.send(h, 1, 0, self.RIGHT, self.to(h, 0, -1), 3)
        for h in range(2):
            self.second_send(h, 1)
            self.second_send(h, 2)
            self.sibling(h, 1, 0)
            self.sibling(h, 2, 0)

    def first_last(self):
        for h in range(2):
            self.recv(h, 2, 0, self.LEFT, 2)
            self.recv(h, 2, 0, self.RIGHT, 3)
            self.second_send(h, 3)
            self.sibling(h, 3, 0)

    def second_send(self, h, ii):
        i = self.OFF[ii]
        self.send(h, i, 0, self.ALL, self.to(h, 1, 1), 4 + 2 * ii)
        self.send(h, i, 0, self.ALL, self.to(h, 1, -1), 5 + 2 * ii)

    def second_recv(self, ii):
        i = self.OFF[ii]
        for h in range(2):
            self.recv(h, i, -1, self.ALL, 4 + 2 * ii)
            self.send(h, i, -1, self.LEFT, self.to(h, 1, 1), 12 + 2 * ii)
            self.recv(h, i, 1, self.ALL, 5 + 2 * ii)
            self.send(h, i, 1, self.RIGHT, self.to(h, 1, -1), 13 + 2 * ii)
            self.sibling(h, ii, 1)
            self.sibling(h, ii, 2)

    def second_last(self, ii):
        i = self.OFF[ii]
        for h in range(2):
            self.recv(h, i, 2, self.LEFT, 12 + 2 * ii)
            self.recv(h, i, 2, self.RIGHT, 13 + 2 * ii)
            self.sibling(h, ii, 3)

    def whole(self, blocks):
        x, y, z, c = self.me
        ref = self.buf.at[pl.ds(0, blocks)]
        return rcopy(ref, ref, self.ssem, self.csem, device(x, y, z, 1 - c))

    def finish(self):
        self.whole(16).wait_recv()

    def drain(self):
        self.whole(31).wait_send()


class Ring:
    LONG = {1: (0, 1), -1: (2, 3)}

    def __init__(self, buf, slot, me, ssem, rsem):
        self.buf, self.slot, self.me = buf, slot, me
        self.ssem, self.rsem = ssem, rsem

    def order(self, k):
        lo, sh = self.LONG[1], self.LONG[-1]
        if k == 4:
            return ((1, lo[0]), (-1, sh[0]), (1, lo[1]), (-1, sh[1]))
        return ((1, lo[0]), (-1, sh[0]), (1, sh[0]), (-1, lo[0]),
                (1, lo[1]), (-1, sh[1]), (1, sh[1]), (-1, lo[1]))

    def view(self, origin, part):
        return self.buf.at[self.slot(lax.rem(origin + 16, 8)), pl.ds(80 * part, 80)]

    def send(self, way, part, k, src=None):
        x, y, z, c = self.me
        d = 0 if way > 0 else 1
        ref = self.view(z - way * (k - 1), part)
        rcopy(ref if src is None else src, ref, self.ssem,
              self.rsem.at[d, part, k - 1], device(x, y, z + way, c)).start()

    def recv(self, way, part, k):
        x, y, z, c = self.me
        d = 0 if way > 0 else 1
        ref = self.view(z - way * k, part)
        rcopy(ref, ref, self.ssem, self.rsem.at[d, part, k - 1],
              device(x, y, z + way, c)).wait_recv()
        if k < 3 or (k == 3 and part in self.LONG[way]):
            self.send(way, part, k + 1)

    def drain(self):
        x, y, z, c = self.me
        ref = self.buf.at[pl.ds(0, 7)]
        rcopy(ref, ref, self.ssem, self.rsem.at[0, 0, 0], device(x, y, z + 1, c)).wait_send()


def mega(tok_in, q_in, kv0_in, out_in, kv1_in, dest_in, len_in, gains_in, qg_in, kg_in,
         cos_in, sin_in, mask_in, lanes_in, caches,
         XS, KV0, KV1, DEST, LEN, gains, qg, kg, cos, sin, mask, lanes, land0, land1, info_land, OUT,
         WQS, WOS, XX, WQ, WO, A, ACC, HID, HB, PP, RSS, RSR, SS, SEND0, SEND1, VAL, INFO, MY, XN,
         in_sem, own_sem, out_sem, swap_s, swap_r, xs, xr, xcs, xcr, wqs, wqr, wqc, ts, tr, wos, wor, woc,
         as_, ar, rss, rsr, sss, ssr, es, er, fs, fr, ns, nr):
    e = lax.axis_index("engine")
    t = lax.axis_index("tensor")
    x, y, a = e // 8, lax.rem(e, 4), lax.rem(e // 4, 2)
    zl, c = t // 2, lax.rem(t, 2)
    z = a * 4 + zl
    me = (x, y, z, c)
    sib = device(x, y, z, 1 - c)
    partner = device(x, y, z + 4, 1 - c)
    moved = a != c

    def t_to(u):
        return device(x, zl + 1, a * 4 + 2 * u + lax.rem(y, 2), c)

    def t_from(yhi):
        return device(x, 2 * yhi + lax.rem(zl, 2), a * 4 + mod4(y - 1), c)

    bar = pltpu.get_barrier_semaphore()
    for other in (device(x + 1, y, z, c), device(x - 1, y, z, c), device(x, y + 1, z, c),
                  device(x, y - 1, z, c), device(x, y, z + 1, c), device(x, y, z - 1, c),
                  sib, partner, t_to(0), t_to(1), t_from(0), t_from(1)):
        pl.semaphore_signal(bar, inc=1, device_id=other, device_id_type=MESH)

    def x_slot(origin):
        oa, ol = origin // 4, lax.rem(origin, 4)
        return jnp.where(oa == c, 2 * ol + c, 8 + ol)

    ring = Ring(XX, x_slot, me, xs, xr)
    own_x = pltpu.make_async_copy(XS, XX.at[x_slot(z)], own_sem.at[2])

    def x_first():
        for way, part in ring.order(1):
            ring.send(way, part, 1, XS.at[pl.ds(80 * part, 80)])
        own_x.start()

    fetch = {}
    for n, (src, dst) in enumerate((
            (tok_in, XS), (kv0_in, KV0), (dest_in, DEST), (len_in, LEN), (kv1_in, KV1),
            (gains_in, gains), (qg_in, qg), (kg_in, kg), (cos_in, cos), (sin_in, sin),
            (mask_in, mask), (lanes_in, lanes))):
        fetch[n] = pltpu.make_async_copy(src, dst, in_sem.at[n])
        fetch[n].start()
    q_copy = pltpu.make_async_copy(q_in, WQS.at[:, pl.ds(0, 512)], own_sem.at[0])
    out_copy = pltpu.make_async_copy(out_in, WOS.at[:, pl.ds(0, 512)], own_sem.at[1])
    q_copy.start()
    out_copy.start()
    for n in (1, 2, 3):
        fetch[n].wait()
    for kind in range(2):
        WQS[:, 512 + 128 * kind:640 + 128 * kind] = KV0[:, kind, :]
    MY[...] = jnp.zeros_like(MY)
    MY[:, 0:16] = DEST[...]
    MY[:, 16:32] = LEN[...]
    q_copy.wait()
    fetch[0].wait()
    pl.semaphore_wait(bar, 12)

    def wq_slot(sx, sy, sc):
        return sx * 8 + sc * 4 + sy

    def wo_slot(sx, sy, sc):
        return (2 * mod4(sy - 1) + sc) * 4 + sx

    swap_slot = x * 8 + a * 4 + y

    def swap_copies():
        return (
            rcopy(WQS, WQ.at[swap_slot], swap_s.at[0], swap_r.at[0], partner),
            rcopy(MY, INFO, swap_s.at[1], swap_r.at[1], partner),
        )

    def stay_copies():
        return (
            pltpu.make_async_copy(WQS, WQ.at[swap_slot], swap_r.at[0]),
            pltpu.make_async_copy(MY, INFO, swap_r.at[1]),
        )

    gq = Gather(WQ, wq_slot, me, wqs, wqr, wqc)

    @pl.when(moved)
    def _():
        for cp in swap_copies():
            cp.start()

    @pl.when(jnp.logical_not(moved))
    def _():
        for cp in stay_copies():
            cp.start()

    x_first()

    @pl.when(jnp.logical_not(moved))
    def _():
        for cp in stay_copies():
            cp.wait()
        gq.first()

    def x_cross(origin, part, src=None):
        origin = lax.rem(origin + 16, 8)
        oa, ol = origin // 4, lax.rem(origin, 4)

        @pl.when(oa != c)
        def _():
            rows = pl.ds(80 * part, 80)
            rcopy(XX.at[8 + ol, rows] if src is None else src, XX.at[2 * ol + c, rows],
                  xcs, xcr.at[ol], sib).start()

    def x_crossed(ol):
        rcopy(XX.at[8 + ol], XX.at[2 * ol + 1 - c], xcs, xcr.at[ol], sib).wait_recv()

    def x_recv(k, low=0, high=8):
        for way, part in ring.order(k)[low:high]:
            ring.recv(way, part, k)
            x_cross(z - way * k, part)

    for part in range(4):
        x_cross(z, part, XS.at[pl.ds(80 * part, 80)])

    fetch[4].wait()
    for kind in range(2):
        WOS[:, 512 + 128 * kind:640 + 128 * kind] = KV1[:, kind, :]
    def moved_first():
        @pl.when(moved)
        def _():
            for cp in swap_copies():
                cp.wait()
            gq.first()


    def shift(u):
        return rcopy(WOS.at[pl.ds(80 * u, 80)],
                     WO.at[(2 * zl + c) * 4 + x, pl.ds(80 * (y // 2), 80)],
                     ts, tr.at[y // 2], t_to(u))

    def shift_start():
        out_copy.wait()
        for u in range(2):
            shift(u).start()

    def shift_recv():
        for yhi in range(2):
            half = WO.at[wo_slot(x, y, c), pl.ds(80 * yhi, 80)]
            rcopy(half, half, ts, tr.at[yhi], sib).wait_recv()

    go = Gather(WO, wo_slot, me, wos, wor, woc)
    moved_first()
    x_recv(1, 0, 4)
    gq.first_recv()
    x_recv(1, 4, 8)
    gq.first_last()
    x_recv(2, 0, 4)
    gq.second_recv(0)
    gq.second_recv(1)
    x_recv(2, 4, 8)
    shift_start()
    gq.second_recv(2)
    gq.second_last(0)
    x_recv(3, 0, 4)
    gq.second_recv(3)
    gq.second_last(1)
    gq.second_last(2)
    x_recv(3, 4, 8)
    gq.second_last(3)
    shift_recv()
    go.first()
    own_x.wait()
    for n in range(5, 12):
        fetch[n].wait()

    def scale_step(i, total):
        xv = XX[i].astype(F32)
        gain = gains[0:1, pl.ds(pl.multiple_of(640 * i, 128), 640)]
        XN[i] = (xv * gain).astype(BF)
        return total + jnp.sum(xv * xv, axis=1, keepdims=True)

    def qkv_step(i, carry):
        w = WQ[pl.ds(4 * i, 4)].reshape(640, WC)
        ACC[...] += jnp.dot(XN[i], w, preferred_element_type=F32)
        return carry

    def chunk(j):
        return 2 * lax.rem(zl + 1 + j // 2, 4) + lax.rem(j, 2)

    ACC[...] = jnp.zeros_like(ACC)
    for n in range(1, 4):
        x_crossed(lax.rem(zl + n, 4))
    total = lax.fori_loop(0, 6, lambda j, s: scale_step(chunk(j), s), jnp.zeros((TOK, 1), F32))
    x_recv(4, 0, 4)
    gq.finish()
    lax.fori_loop(0, 3, lambda j, s: qkv_step(chunk(j), s), 0)
    go.first_recv()
    lax.fori_loop(3, 6, lambda j, s: qkv_step(chunk(j), s), 0)
    x_crossed(zl)
    total = lax.fori_loop(6, 8, lambda j, s: scale_step(chunk(j), s), total)
    lax.fori_loop(6, 8, lambda j, s: qkv_step(chunk(j), s), 0)
    r0 = lax.rsqrt(total / 5120.0 + EPS)
    cosv, sinv = cos[...], sin[...]
    VAL[:, 0:128] = rope(head_norm(ACC[:, 512:640] * r0, kg[0:1]), cosv, sinv).astype(BF)
    VAL[:, 128:256] = (ACC[:, 640:768] * r0).astype(BF)
    for g in range(4):
        cols = slice(128 * g, 128 * g + 128)
        A[z, :, cols] = rope(head_norm(ACC[:, cols] * r0, qg[...]), cosv, sinv).astype(BF)
    go.first_last()
    att = Ring(A, lambda origin: origin, me, as_, ar)
    for n in (0, 2, 1, 3):
        rows = slice(CB * n, CB * n + CB)
        keys = slice(0, CB * n + CB)
        q = jnp.concatenate([A[z, rows, 128 * g:128 * g + 128] for g in range(4)], axis=0)
        s = lax.dot_general(q, VAL[keys, 0:128], NT, preferred_element_type=F32)
        seen = jnp.concatenate([mask[rows, keys]] * 4, axis=0)
        w = jnp.where(seen > 0, jnp.exp(s / jnp.sqrt(F32(128.0))), 0.0)
        p = (w / jnp.sum(w, axis=1, keepdims=True)).astype(BF)
        o = jnp.dot(p, VAL[keys, 128:256], preferred_element_type=F32).astype(BF)
        for g in range(4):
            A[z, rows, 128 * g:128 * g + 128] = o[CB * g:CB * g + CB]
        att.send(1, n, 1)
        att.send(-1, n, 1)

    def att_recv(k, low=0, high=8):
        for way, part in att.order(k)[low:high]:
            att.recv(way, part, k)

    def go_second_recv_0():
        go.second_recv(0)

    info = jnp.broadcast_to(INFO[...].astype(F32), (8, 128)).astype(BF)
    lane = lax.broadcasted_iota(jnp.int32, (128, TOK), 0)
    row_of, tok_of = lanes[0:1, :], lanes[1:2, :]
    dest_l = jnp.dot(info, (lane == row_of).astype(BF), preferred_element_type=F32)[0:1]
    len_l = jnp.dot(info, (lane == row_of + 16).astype(BF), preferred_element_type=F32)[0:1]
    dest_l = dest_l.astype(jnp.int32)
    live = tok_of < len_l.astype(jnp.int32)
    key_a = jnp.where(jnp.logical_and(live, tok_of < 16), dest_l * 16 + tok_of, -1000)
    key_b = jnp.where(jnp.logical_and(live, tok_of >= 16), dest_l * 16 + tok_of - 16, -1000)
    place = lax.broadcasted_iota(jnp.int32, (512, TOK), 0)

    def head_rows(cols):
        return jnp.dot((place == key_a).astype(BF), VAL[:, cols], preferred_element_type=F32)

    def tail_rows(f):
        return jnp.dot((place == key_b + 4 * f).astype(BF), VAL[:, 128 * f:128 * f + 128],
                       preferred_element_type=F32)

    g1, tails = [], []

    def prep():
        SEND0[...] = head_rows(slice(0, 256)).astype(BF).reshape(32, 16, 256)
        tail = tail_rows(0) + tail_rows(1)
        SEND1[:, :, 256:384] = tail.astype(BF).reshape(32, 16, 128)
        tails.append(tail)
        pick_row = lax.broadcasted_iota(jnp.int32, (640, 160), 0)
        pick_col = lax.broadcasted_iota(jnp.int32, (640, 160), 1)
        u, v = zl // 2, lax.rem(zl, 2)
        pick = pick_row == pick_col + jnp.where(pick_col >= 80, 240, 0) + (160 * v + 80 * u)
        pick_b, pick_f = pick.astype(BF), pick.astype(F32)
        for sx in range(4):
            HID[sx] = jnp.dot(XX[2 * sx + a], pick_b, preferred_element_type=F32)
            at = 1280 * sx
            gv = jnp.where(a == 0, gains[1:2, at:at + 640], gains[1:2, at + 640:at + 1280])
            g1.append(jnp.dot(jnp.broadcast_to(gv, (8, 640)), pick_f, preferred_element_type=F32,
                              precision=lax.Precision.HIGHEST)[0:1])

    mine = x * 8 + c * 4 + y

    def target(d):
        return (d, 2 * zl + a)

    def same(d):
        return jnp.logical_and(d == e, a == c)

    def hand_out(srcs):
        def step(d, carry):

            @pl.when(same(d))
            def _():
                for src, dst, ss, rs in srcs(d):
                    pltpu.make_async_copy(src, dst, rs).start()

            @pl.when(jnp.logical_not(same(d)))
            def _():
                for src, dst, ss, rs in srcs(d):
                    rcopy(src, dst, ss, rs, target(d)).start()
            return carry

        lax.fori_loop(0, 32, step, 0)

    def early(d):
        return ((INFO, info_land.at[mine], ns, nr), (SEND0.at[d], land0.at[mine], es, er))

    def late(d):
        return ((SEND1.at[d], land1.at[mine], fs, fr),)

    def out_step(origin):
        origin = lax.rem(origin + 16, 8)
        head = 2 * lax.rem(origin, 4) + origin // 4
        for sx in range(4):
            part = lax.dot_general(A[origin], WO[head * 4 + sx, :, 0:512], NT,
                                   preferred_element_type=F32)
            HID[sx] += part.astype(BF).astype(F32)

    go_second_recv_0()
    att_recv(1, 0, 2)
    go.second_recv(1)
    att_recv(1, 2, 8)
    go.second_recv(2)
    prep()
    att_recv(2, 0, 2)
    go.second_last(0)
    att_recv(2, 2, 4)
    go.second_recv(3)
    att_recv(2, 4, 8)
    go.second_last(1)
    go.second_last(2)
    att_recv(3, 0, 2)
    go.second_last(3)
    att_recv(3, 2, 8)
    go.finish()
    for k in (0, -1, 1, -2, 2, -3, 3):
        out_step(z + k)
    hand_out(early)
    att_recv(4, 0, 4)
    out_step(z + 4)


    col = jnp.zeros((TOK, 1), F32)
    for sx in range(4):
        hv = HID[sx]
        col = col + jnp.sum(hv * hv, axis=1, keepdims=True)
        HB[sx] = (hv * g1[sx]).astype(BF)

    def partial(dest):
        dest = lax.rem(dest + 16, 8)
        head = 2 * lax.rem(dest, 4) + dest // 4
        out = jnp.dot(HB[0], WO[head * 4, :, 512:768], preferred_element_type=F32)
        for sx in range(1, 4):
            out = out + jnp.dot(HB[sx], WO[head * 4 + sx, :, 512:768], preferred_element_type=F32)
        PP[dest] = out

    def rs_at(way, part, s):
        d = 0 if way > 0 else 14
        long = Ring.LONG[way]
        return d + (4 * long.index(part) + s if part in long else 8 + 3 * Ring.LONG[-way].index(part) + s)

    def rs_copy(way, part, s):
        n = rs_at(way, part, s)
        return rcopy(RSS.at[n], RSR.at[n], rss, rsr.at[n], device(x, y, z + way, c))

    def rs_send(way, part, s, value):
        RSS[rs_at(way, part, s)] = value.astype(BF)
        rs_copy(way, part, s).start()

    def rs_recv(way, part, s):
        rs_copy(way, part, s).wait_recv()
        return RSR[rs_at(way, part, s)].astype(F32)

    def hops(way, part):
        return 4 if part in Ring.LONG[way] else 3

    def own_part(way, part, s):
        dest = lax.rem(z + way * (hops(way, part) - s) + 16, 8)
        return PP[dest, pl.ds(80 * part, 80)]

    partial(z + 4)
    for way, part in ((1, 0), (-1, 2), (1, 1), (-1, 3)):
        rs_send(way, part, 0, own_part(way, part, 0))
    partial(z + 3)
    partial(z - 3)
    for way, part in ((1, 2), (-1, 0), (1, 3), (-1, 1)):
        rs_send(way, part, 0, own_part(way, part, 0))
    eye = (lax.broadcasted_iota(jnp.int32, (TOK, TOK), 0)
           == lax.broadcasted_iota(jnp.int32, (TOK, TOK), 1))
    SS[z] = jnp.sum(jnp.where(eye, col, 0.0), axis=0, keepdims=True)
    for k in range(1, 8):
        rcopy(SS.at[z], SS.at[z], sss, ssr, device(x, y, z + k, c)).start()
    for k in (2, -2, 1, -1, 0):
        partial(z + k)
    ring_order = ((1, 0), (-1, 2), (1, 1), (-1, 3), (1, 2), (-1, 0), (1, 3), (-1, 1))
    for s in range(3):
        for way, part in ring_order:
            if s < hops(way, part) - 1:
                rs_send(way, part, s + 1, rs_recv(way, part, s) + own_part(way, part, s + 1))
    rcopy(SS.at[pl.ds(0, 7)], SS.at[pl.ds(0, 7)], sss, ssr, sib).wait_recv()
    ss_total = SS[0]
    for k in range(1, 8):
        ss_total = ss_total + SS[k]
    r1 = lax.rsqrt(jnp.sum(jnp.where(eye, ss_total, 0.0), axis=1, keepdims=True) / 5120.0 + EPS)

    for part in range(4):
        way = 1 if part in Ring.LONG[1] else -1
        rows = slice(80 * part, 80 * part + 80)
        kv = PP[z, rows] + rs_recv(-way, part, 2) + rs_recv(way, part, 3)
        kv = kv * r1[rows]
        VAL[rows, 256:384] = rope(head_norm(kv[:, 0:128], kg[1:2]), cos[rows], sin[rows]).astype(BF)
        VAL[rows, 384:512] = kv[:, 128:256].astype(BF)

    SEND1[:, :, 0:256] = head_rows(slice(256, 512)).astype(BF).reshape(32, 16, 256)
    tail = tails[0] + tail_rows(2) + tail_rows(3)
    SEND1[:, :, 256:384] = tail.astype(BF).reshape(32, 16, 128)
    hand_out(late)

    def landed(groups):
        for dst, ss, rs in groups:
            rcopy(dst, dst, ss, rs, sib).wait_recv()

            @pl.when(a == c)
            def _(dst=dst, ss=ss, rs=rs):
                most = dst.at[pl.ds(0, 31)]
                rcopy(most, most, ss, rs, sib).wait_send()

            @pl.when(a != c)
            def _(dst=dst, ss=ss, rs=rs):
                rcopy(dst, dst, ss, rs, sib).wait_send()

    for part in (ring, gq, go, att):
        part.drain()
    rcopy(RSS, RSS, rss, rsr.at[0], sib).wait_send()
    rcopy(SS.at[pl.ds(0, 7)], SS.at[pl.ds(0, 7)], sss, ssr, sib).wait_send()
    rcopy(WOS, WOS, ts, tr.at[0], sib).wait_send()
    rcopy(XX.at[pl.ds(0, 4)], XX.at[pl.ds(0, 4)], xcs, xcr.at[0], sib).wait_send()

    landed(((info_land, ns, nr), (land0, es, er)))
    lane = lax.broadcasted_iota(jnp.int32, (32, 128), 1)
    hit = jnp.logical_and(info_land[...].reshape(32, 128) == e, lane < 16)
    here = jnp.max(hit.astype(F32), axis=1, keepdims=True)
    before = (lax.broadcasted_iota(jnp.int32, (32, 32), 1)
              < lax.broadcasted_iota(jnp.int32, (32, 32), 0)).astype(BF)
    rank = jnp.dot(before, jnp.broadcast_to(here, (32, 128)).astype(BF), preferred_element_type=F32)
    key = jnp.where(here > 0, rank[:, 0:1], -1000.0)
    key = jnp.broadcast_to(key[:, None, :], (32, 16, 512))
    row = lax.broadcasted_iota(jnp.int32, (32, 16, 512), 1).astype(F32) * 32.0
    at = lax.broadcasted_iota(jnp.int32, (32, 16, 512), 2).astype(F32)
    pick_rows = (key + row == at).astype(BF).reshape(512, 512)
    tn = (((0,), (0,)), ((), ()))

    def settle(block):
        out = lax.dot_general(pick_rows, block, tn, preferred_element_type=F32)
        return out.astype(BF).reshape(16, 32, block.shape[1])

    rows0 = settle(land0[...].reshape(512, 256))
    for f in range(2):
        OUT[f, 0:16] = rows0[:, :, 128 * f:128 * f + 128]
    landed(((land1, fs, fr),))
    rows1 = settle(land1[...].reshape(512, 384))
    for f in range(2):
        OUT[2 + f, 0:16] = rows1[:, :, 128 * f:128 * f + 128]
    for f in range(4):
        OUT[f, 16:20] = rows1[4 * f:4 * f + 4, :, 256:384]
    put = pltpu.make_async_copy(OUT, caches, out_sem)
    put.start()
    put.wait()


def tables():
    half = 64
    where = np.arange(TOK) // 16
    pos = where.astype(np.float32)
    freq = np.power(ROTARY_BASE, -np.arange(half, dtype=np.float64) * 2.0 / 128).astype(np.float32)
    angle = (pos[:, None] * freq[None, :]).astype(np.float32).astype(np.float64)
    cos, sin = np.cos(angle), np.sin(angle)
    cos = np.concatenate([cos, cos], axis=1).astype(np.float32)
    sin = np.concatenate([-sin, sin], axis=1).astype(np.float32)
    i, j = np.arange(TOK)[:, None], np.arange(TOK)[None, :]
    mask = ((i % 16 == j % 16) & (j <= i)).astype(np.float32)
    lanes = np.zeros((8, TOK), np.int32)
    lanes[0] = np.arange(TOK) % 16
    lanes[1] = where
    return cos, sin, mask, lanes


def body(token_states, row_len, row_dest, norm_gain, q_gain, k_gain,
         q_weight, kv_weight0, out_weight, kv_weight1):
    cos, sin, mask, lanes = tables()
    hbm = pl.BlockSpec(memory_space=pl.ANY)
    dma = pltpu.SemaphoreType.DMA
    vmem = pltpu.VMEM
    out = pl.pallas_call(
        mega,
        out_shape=jax.ShapeDtypeStruct((4, SPAN, 32, 128), BF),
        in_specs=[hbm] * 14,
        out_specs=hbm,
        scratch_shapes=[
            vmem((TOK, 640), BF), vmem((160, 2, 128), BF), vmem((160, 2, 128), BF),
            vmem((1, 16), jnp.int32), vmem((1, 16), jnp.int32),
            vmem((2, 5120), F32), vmem((1, 128), F32), vmem((2, 128), F32),
            vmem((TOK, 128), F32), vmem((TOK, 128), F32), vmem((TOK, TOK), F32), vmem((8, TOK), jnp.int32),
            vmem((32, 16, 256), BF), vmem((32, 16, 384), BF), vmem((32, 1, 128), jnp.int32),
            vmem((4, SPAN, 32, 128), BF),
            vmem((160, WC), BF), vmem((160, WC), BF),
            vmem((12, TOK, 640), BF), vmem((32, 160, WC), BF), vmem((32, 160, WC), BF),
            vmem((8, TOK, 512), BF), vmem((TOK, WC), F32),
            vmem((4, TOK, 160), F32), vmem((4, TOK, 160), BF), vmem((8, TOK, 256), F32),
            vmem((28, 80, 256), BF), vmem((28, 80, 256), BF), vmem((8, 1, TOK), F32),
            vmem((32, 16, 256), BF), vmem((32, 16, 384), BF), vmem((TOK, 512), BF),
            vmem((1, 128), jnp.int32), vmem((1, 128), jnp.int32), vmem((8, TOK, 640), BF),
            dma((12,)), dma((3,)), dma, dma((2,)), dma((2,)),
            dma, dma((2, 4, 4)), dma, dma((4,)),
            dma, dma((2, 20)), dma, dma, dma((2,)), dma, dma((2, 20)), dma,
            dma, dma((2, 4, 4)), dma, dma((28,)),
            dma, dma, dma, dma, dma, dma, dma, dma,
        ],
        compiler_params=pltpu.CompilerParams(
            collective_id=0, has_side_effects=True, vmem_limit_bytes=58 * 2**20),
        name="prefill",
    )(token_states.transpose(1, 0, 2).reshape(TOK, 640), q_weight, kv_weight0, out_weight, kv_weight1,
      row_dest.reshape(1, 16), row_len.reshape(1, 16),
      norm_gain, q_gain.reshape(1, 128), k_gain,
      jnp.asarray(cos), jnp.asarray(sin), jnp.asarray(mask), jnp.asarray(lanes))
    return out.reshape(2, 2, SPAN, 32, 128).transpose(0, 1, 3, 2, 4)


def solution(mesh):
    in_specs = (
        P("engine", None, "tensor"), P("engine"), P("engine"), P(), P(), P(),
        P("engine", "tensor"), P("engine", None, "tensor"),
        P("engine", "tensor"), P("engine", None, "tensor"),
    )
    out_specs = P(None, None, "engine", None, "tensor")
    return jax.shard_map(body, mesh=mesh, in_specs=in_specs, out_specs=out_specs, check_vma=False)
```
